768 devices in a mesh: rows: 96 (over z, x, core), rep: 8 (over y).
Axes of the slice: x: 4, y: 8, z: 12, core: 2. Of those that a mesh axis runs over, the one named last changes fastest.
Arguments:
- block_values: bfloat16 [1536, 8, 64, 64], P('rows'), may hold values from -0.8984375 to 0.8984375
- pattern_cols: int32 [1536, 8], replicated, may hold values from 0 to 1535, as said below
- pattern_counts: int32 [1536], replicated, may hold values from 4 to 8, as said below
Outputs:
- purified: bfloat16 [1536, 8, 64, 64], P('rows', 'rep')
The draws below stay inside these ranges and needn't reach their ends.
Inputs may be any that keep to these rules, and one draw needn't show every extreme that they name: `pattern_cols`: slot 0 of block row i holds i, slot 1 holds i + 8 or i - 8 modulo 1536, every column of row i lies within 8 of i modulo 1536, and the columns of a row are distinct. Only slots below pattern_counts[i] hold blocks of the matrix; some block row uses all 8 slots.
All inputs are finite; a program needn't handle non-finite values.
Results may differ from the reference program's by a relative error of at most 0.0049.
Values may be sent and summed in bfloat16 or wider, within the bound.
No kernel may reach another device: no remote copies, remote signals or barrier semaphores. Data moves between devices by JAX's collectives and lax.ppermute only.
A program may use at most 32 MiB of HBM per device.

```python
import jax
import jax.numpy as jnp
from jax import lax

BS = 64
K = 8
BR_DEV = 16
SPAN = 8
NBLK = 1536


def draw_pattern_cols(key, part):
    first_key = jax.random.fold_in(key, 11)
    second_key = jax.random.fold_in(key, 12)
    pool_size = 2 * SPAN - 2
    signs = jax.random.randint(first_key, (NBLK,), 0, 2).astype(jnp.int32) * 2 - 1
    offsets_pool = jnp.concatenate([jnp.arange(1 - SPAN, 0, dtype=jnp.int32), jnp.arange(1, SPAN, dtype=jnp.int32)])
    scores = jax.random.randint(second_key, (NBLK, pool_size), 0, 1 << 20).astype(jnp.int32) * pool_size + jnp.arange(pool_size, dtype=jnp.int32)[None, :]
    ordering = jnp.argsort(scores, axis=1, stable=True)[:, :K - 2]
    picked = jnp.take(offsets_pool, ordering, axis=0)
    row_index = jnp.arange(NBLK, dtype=jnp.int32)
    offsets = jnp.concatenate([jnp.zeros((NBLK, 1), jnp.int32), (signs * SPAN)[:, None], picked], axis=1)
    return ((row_index[:, None] + offsets) % NBLK).astype(jnp.int32)


def draw_pattern_counts(key, part):
    first_key = jax.random.fold_in(key, 21)
    second_key = jax.random.fold_in(key, 22)
    counted = jax.random.randint(first_key, (NBLK,), K // 2, K + 1).astype(jnp.int32)
    fullest = jax.random.randint(second_key, (), 0, NBLK).astype(jnp.int32)
    row_index = jnp.arange(NBLK, dtype=jnp.int32)
    return jnp.where(row_index == fullest, K, counted).astype(jnp.int32)


def steps_of(key, extent, split, least, top_value):
    def one(axis_at, parts):
        heights = jax.random.uniform(jax.random.fold_in(jax.random.fold_in(key, 6), axis_at), (parts,), jnp.float32, least / len(split), top_value / len(split))
        return jnp.repeat(jnp.exp(heights), extent[axis_at] // parts).reshape((-1,) + (1,) * (len(extent) - axis_at - 1))

    gain = one(*split[0])
    for cut in split[1:]:
        gain = gain * one(*cut)
    return gain


def gaussian(own_key, extent, deviation, reach, shards=(), kind=jnp.bfloat16):
    entries = jax.random.normal(own_key, extent, jnp.float32) * deviation
    if len(shards) > 0:
        entries = steps_of(own_key, extent, shards, -0.22, 0.18) * entries
    return jnp.clip(entries, min=-reach, max=reach).astype(kind)


def setup_inputs(seed: int = 0) -> dict:
    splits = jax.random.split(jax.random.key(seed), 4)
    return {
        "block_values": gaussian(splits[0], (NBLK, K, BS, BS), 0.15, 0.8984375, ((0, 96),)),
        "pattern_cols": draw_pattern_cols(jax.random.fold_in(splits[3], 71), 0),
        "pattern_counts": draw_pattern_counts(jax.random.fold_in(splits[3], 71), 0),
    }


def lookup(values, pattern_cols, pattern_counts, row_ids, slot_ids, anchor, halo_reach):
    total_rows = pattern_cols.shape[0]
    slot_count = pattern_cols.shape[1]
    block_side = values.shape[-1]
    own_cols = jnp.take(pattern_cols, row_ids, axis=0)
    own_count = jnp.take(pattern_counts, row_ids, axis=0)
    target = jnp.take(own_cols, slot_ids, axis=1)
    far_cols = jnp.take(pattern_cols, own_cols, axis=0)
    far_count = jnp.take(pattern_counts, own_cols, axis=0)
    position = jnp.arange(slot_count, dtype=jnp.int32)
    matched = (far_cols[:, None, :, :] == target[:, :, None, None]) & (position[None, None, None, :] < far_count[:, None, :, None])
    located = jnp.any(matched, axis=3) & (position[None, None, :] < own_count[:, None, None]) & (slot_ids[None, :, None] < own_count[:, None, None])
    where_at = jnp.sum(jnp.where(matched, position[None, None, None, :], 0), axis=3).astype(jnp.int32)
    local_row = ((own_cols - anchor + halo_reach) % total_rows).astype(jnp.int32)
    flat_index = local_row[:, None, :] * slot_count + where_at
    blocks = jnp.take(values.reshape(-1, block_side, block_side), flat_index, axis=0)
    return jnp.where(located[..., None, None], blocks, jnp.zeros((), values.dtype))


def reference(block_values, pattern_cols, pattern_counts):
    total_rows = block_values.shape[0]
    slot_count = block_values.shape[1]
    block_side = block_values.shape[2]
    every_slot = jnp.arange(slot_count, dtype=jnp.int32)

    def one_group(row_ids):
        gathered = lookup(block_values, pattern_cols, pattern_counts, row_ids, every_slot, 0, 0)
        own_rows = jnp.take(block_values, row_ids, axis=0)
        squared = jnp.einsum('gbxy,gabyz->gaxz', own_rows.astype(jnp.float32), gathered.astype(jnp.float32))
        square = lax.optimization_barrier(squared.astype(jnp.bfloat16))
        cube = jnp.einsum('gbxy,gabyz->gaxz', square.astype(jnp.float32), gathered.astype(jnp.float32))
        return (3.0 * square.astype(jnp.float32) - 2.0 * cube).astype(jnp.bfloat16)

    row_groups = jnp.arange(total_rows, dtype=jnp.int32).reshape(-1, BR_DEV)
    result = lax.map(one_group, row_groups)
    return result.reshape(total_rows, slot_count, block_side, block_side)
```

```python
import functools

import jax
import jax.numpy as jnp
from jax import lax
from jax.experimental import pallas as pl
from jax.experimental.pallas import tpu as pltpu
from jax.sharding import PartitionSpec as P

HALF = 8
WINDOW = 32
ZERO_TILE = WINDOW * 8
TABLE_ROWS = WINDOW + 8


def swapped(tile):
    return pltpu.roll(tile, 64, 1)


def pack_kernel(x_ref, near_ref, far_ref):
    core = lax.rem(lax.axis_index("rows"), 2)
    for ref, base in ((near_ref, core * HALF), (far_ref, (1 - core) * HALF)):
        for row in range(HALF):
            for pair in range(4):
                ref[row, pair, :, 0:64] = x_ref[base + row, 2 * pair]
                ref[row, pair, :, 64:128] = x_ref[base + row, 2 * pair + 1]


def table_kernel(cols_ref, counts_ref, out_ref):
    total = cols_ref.shape[1]
    chunks = total // 128
    start = lax.rem(lax.axis_index("rows") * (2 * HALF) + (total - HALF), total)
    first = lax.div(start, 128)
    second = lax.rem(first + 1, chunks)
    offset = lax.rem(start, 128)
    shift = lax.rem(256 - offset, 256)

    def window(get):
        both = jnp.concatenate([get(first), get(second)], axis=1)
        return pltpu.roll(both, shift, 1)[:, :128]

    cols = window(lambda k: cols_ref[:, pl.ds(pl.multiple_of(k * 128, 128), 128)])
    counts = window(lambda k: jnp.broadcast_to(counts_ref[pl.ds(k, 1), :], (8, 128)))
    relative = cols - start
    relative = jnp.where(relative < 0, relative + total, relative)
    slot = lax.broadcasted_iota(jnp.int32, (8, 128), 0)
    lane = lax.broadcasted_iota(jnp.int32, (8, 128), 1)
    live = (slot < counts) & (lane < WINDOW)
    matchable = jnp.where(live & (relative < WINDOW), relative, -1)
    column = lax.broadcasted_iota(jnp.int32, (TABLE_ROWS, 128), 0)
    row = lax.broadcasted_iota(jnp.int32, (TABLE_ROWS, 128), 1)
    tiles = jnp.full((TABLE_ROWS, 128), ZERO_TILE, jnp.int32)
    for s in range(8):
        here = jnp.broadcast_to(matchable[s : s + 1, :], (TABLE_ROWS, 128)) == column
        tiles = jnp.where(here, row * 8 + ((s % 2) * 4 + s // 2), tiles)
    out_ref[0:TABLE_ROWS, :] = tiles
    out_ref[TABLE_ROWS : TABLE_ROWS + 8, :] = jnp.where(live, relative, WINDOW)


def half_kernel(far_half, table_ref, center_ref, other_ref, halo_ref, *refs):
    out_ref, store = refs[-2], refs[-1]
    core = lax.rem(lax.axis_index("rows"), 2)
    mine = lax.axis_index("rep")
    low_halo = core if far_half else 1 - core
    center = 2 - low_halo
    swap = lax.rem(mine, 2)
    pair_of = lax.div(mine, 2)

    zeros = jnp.zeros((64, 128), jnp.bfloat16)
    store[ZERO_TILE] = zeros
    store[ZERO_TILE + 4] = zeros
    for ref, chunk in ((center_ref, center), (other_ref, 3 - center), (halo_ref, 3 * (1 - low_halo))):
        for row in range(HALF):
            base = (chunk * HALF + row) * 8
            for pair in range(4):
                tile = ref[row, pair]
                store[base + pair] = tile
                store[base + 4 + pair] = swapped(tile)

    left = lax.broadcasted_iota(jnp.int32, (64, 128), 1) < 64
    for i in range(HALF):
        at = center * HALF + i
        cols = [table_ref[(TABLE_ROWS + (mine ^ q)) * 128 + at] for q in range(8)]
        x = jnp.concatenate([store[at * 8 + swap * 4 + (pair_of ^ p)] for p in range(4)], axis=1)

        def tile(p, b):
            one = table_ref[cols[2 * p] * 128 + cols[b]]
            two = table_ref[cols[2 * p + 1] * 128 + cols[b]] ^ 4
            return jnp.where(left, store[one], store[two])

        squares = []
        for n in range(2):
            total = None
            for k in range(2):
                g = jnp.concatenate(
                    [
                        jnp.concatenate([tile(2 * n + j, 4 * k + b) for j in range(2)], axis=1)
                        for b in range(4)
                    ],
                    axis=0,
                )
                part = jnp.dot(x[:, k * 256 : (k + 1) * 256], g, preferred_element_type=jnp.float32)
                total = part if total is None else total + part
            squares.append(total.astype(jnp.bfloat16))
        cube = None
        for k in range(2):
            g = jnp.concatenate(
                [store[table_ref[cols[0] * 128 + cols[4 * k + b]]] for b in range(4)], axis=0
            )
            part = jnp.dot(squares[k], g, preferred_element_type=jnp.float32)
            cube = part if cube is None else cube + part
        purified = 3.0 * squares[0][:, :128].astype(jnp.float32) - 2.0 * cube
        out_ref[i, 0] = purified[:, :64].astype(jnp.bfloat16)


def vmem():
    return pl.BlockSpec(memory_space=pltpu.VMEM)


def half(far_half, table, center, other, halo, carried, rows_here):
    def out_block():
        core = lax.rem(lax.axis_index("rows"), 2)
        return ((1 - core) if far_half else core, 0, 0, 0)

    shape = jax.ShapeDtypeStruct((rows_here, 1, 64, 64), jnp.bfloat16)
    extra = [] if carried is None else [carried]
    return pl.pallas_call(
        functools.partial(half_kernel, far_half),
        grid=(1,),
        out_shape=shape,
        in_specs=[pl.BlockSpec(memory_space=pltpu.SMEM)]
        + [vmem()] * 3
        + [pl.BlockSpec(memory_space=pl.ANY)] * len(extra),
        out_specs=pl.BlockSpec((HALF, 1, 64, 64), lambda _: out_block()),
        scratch_shapes=[pltpu.VMEM((ZERO_TILE + 8, 64, 128), jnp.bfloat16)],
        input_output_aliases={4: 0} if extra else {},
        compiler_params=pltpu.CompilerParams(vmem_limit_bytes=32 * 1024 * 1024),
        cost_estimate=pl.CostEstimate(flops=600_000_000, bytes_accessed=2_000_000, transcendentals=0),
        name="far_half" if far_half else "near_half",
    )(table, center, other, halo, *extra)


def local(block_values, pattern_cols, pattern_counts):
    rows_here = block_values.shape[0]
    count = lax.axis_size("rows")
    to_core = [(i, i ^ 1) for i in range(count)]
    to_chip = [(i, (i + 1 if i % 2 else i - 1) % count) for i in range(count)]
    packed = jax.ShapeDtypeStruct((HALF, 4, 64, 128), jnp.bfloat16)
    near, far = pl.pallas_call(
        pack_kernel,
        out_shape=(packed, packed),
        in_specs=[vmem()],
        out_specs=(vmem(), vmem()),
        compiler_params=pltpu.CompilerParams(vmem_limit_bytes=32 * 1024 * 1024),
        name="pack",
    )(block_values)
    near_halo = lax.ppermute(near, "rows", to_chip)
    far_halo = lax.ppermute(far, "rows", to_core)
    table = pl.pallas_call(
        table_kernel,
        out_shape=jax.ShapeDtypeStruct((TABLE_ROWS + 8, 128), jnp.int32),
        in_specs=[vmem(), vmem()],
        out_specs=vmem(),
        name="table",
    )(pattern_cols.T, pattern_counts.reshape(-1, 128)).reshape(-1)
    result = half(True, table, far, near, far_halo, None, rows_here)
    return half(False, table, near, far, near_halo, result, rows_here)


def solution(mesh):
    in_specs = (P("rows", None, None, None), P(), P())
    out_specs = P("rows", "rep", None, None)
    return jax.shard_map(local, mesh=mesh, in_specs=in_specs, out_specs=out_specs, check_vma=False)
```

```python
import functools

import jax
import jax.numpy as jnp
from jax import lax
from jax.experimental import pallas as pl
from jax.experimental.pallas import tpu as pltpu
from jax.sharding import PartitionSpec as P

HALF = 8
WINDOW = 32
ZERO_TILE = WINDOW * 8
TABLE_ROWS = WINDOW + 8
TILE = 64
PAD = 16


def swapped(tile):
    return pltpu.roll(tile, 64, 1)


def pack_half(base, x_ref, out_ref, rows, sems):
    copies = [
        pltpu.make_async_copy(x_ref.at[base + row], rows.at[row], sems.at[row])
        for row in range(HALF)
    ]
    for copy in copies:
        copy.start()
    for row in range(HALF):
        copies[row].wait()
        for pair in range(4):
            at = pl.ds((row * 4 + pair) * TILE, TILE)
            out_ref[at, 0:64] = rows[row, 2 * pair]
            out_ref[at, 64:128] = rows[row, 2 * pair + 1]


def near_kernel(x_ref, out_ref, rows, sems):
    core = lax.rem(lax.axis_index("rows"), 2)
    out_ref[HALF * 4 * TILE :, :] = jnp.zeros((PAD, 128), jnp.bfloat16)
    pack_half(core * HALF, x_ref, out_ref, rows, sems)


def far_kernel(x_ref, cols_ref, counts_ref, _, out_ref, table_ref, rows, sems):
    core = lax.rem(lax.axis_index("rows"), 2)
    make_table(cols_ref, counts_ref, table_ref)
    pack_half((1 - core) * HALF, x_ref, out_ref, rows, sems)


def make_table(cols_ref, counts_ref, out_ref):
    total = cols_ref.shape[1]
    chunks = total // 128
    start = lax.rem(lax.axis_index("rows") * (2 * HALF) + (total - HALF), total)
    first = lax.div(start, 128)
    second = lax.rem(first + 1, chunks)
    offset = lax.rem(start, 128)
    shift = lax.rem(256 - offset, 256)

    def window(get):
        both = jnp.concatenate([get(first), get(second)], axis=1)
        return pltpu.roll(both, shift, 1)[:, :128]

    cols = window(lambda k: cols_ref[:, pl.ds(pl.multiple_of(k * 128, 128), 128)])
    counts = window(lambda k: jnp.broadcast_to(counts_ref[pl.ds(k, 1), :], (8, 128)))
    relative = cols - start
    relative = jnp.where(relative < 0, relative + total, relative)
    slot = lax.broadcasted_iota(jnp.int32, (8, 128), 0)
    lane = lax.broadcasted_iota(jnp.int32, (8, 128), 1)
    live = (slot < counts) & (lane < WINDOW)
    matchable = jnp.where(live & (relative < WINDOW), relative, -1)
    column = lax.broadcasted_iota(jnp.int32, (TABLE_ROWS, 128), 0)
    row = lax.broadcasted_iota(jnp.int32, (TABLE_ROWS, 128), 1)
    tiles = jnp.full((TABLE_ROWS, 128), ZERO_TILE, jnp.int32)
    for s in range(8):
        here = jnp.broadcast_to(matchable[s : s + 1, :], (TABLE_ROWS, 128)) == column
        tiles = jnp.where(here, row * 8 + ((s % 2) * 4 + s // 2), tiles)
    out_ref[0:TABLE_ROWS, :] = tiles
    out_ref[TABLE_ROWS : TABLE_ROWS + 8, :] = jnp.where(live, relative, WINDOW)


def half_kernel(far_half, table_in, center_ref, other_ref, halo_ref, *refs):
    out_ref, store, table_ref, squares_ref, sem = refs[-5:]
    fetch = pltpu.make_async_copy(table_in, table_ref, sem)
    fetch.start()
    core = lax.rem(lax.axis_index("rows"), 2)
    mine = lax.axis_index("rep")
    low_halo = core if far_half else 1 - core
    center = 2 - low_halo
    swap = lax.rem(mine, 2)
    pair_of = lax.div(mine, 2)

    zeros = jnp.zeros((64, 128), jnp.bfloat16)
    store[ZERO_TILE] = zeros
    store[ZERO_TILE + 4] = zeros
    for ref, chunk in ((center_ref, center), (other_ref, 3 - center), (halo_ref, 3 * (1 - low_halo))):
        for row in range(HALF):
            base = (chunk * HALF + row) * 8
            for pair in range(4):
                tile = ref[pl.ds((row * 4 + pair) * TILE, TILE), :]
                store[base + pair] = tile
                store[base + 4 + pair] = swapped(tile)
    fetch.wait()

    left = lax.broadcasted_iota(jnp.int16, (64, 128), 1) < 64
    columns = [
        [table_ref[TABLE_ROWS + (mine ^ q), center * HALF + i] for q in range(8)] for i in range(HALF)
    ]
    for i in range(HALF):
        cols = columns[i]
        at = (center * HALF + i) * 8 + swap * 4
        x = jnp.concatenate([store[at + (pair_of ^ p)] for p in range(4)], axis=1)

        def tile(p, b):
            one = table_ref[cols[2 * p], cols[b]]
            two = table_ref[cols[2 * p + 1], cols[b]] ^ 4
            return jnp.where(left, store[one], store[two])

        for n in range(2):
            total = None
            for k in range(2):
                g = jnp.concatenate(
                    [
                        jnp.concatenate([tile(2 * n + j, 4 * k + b) for j in range(2)], axis=1)
                        for b in range(4)
                    ],
                    axis=0,
                )
                part = jnp.dot(x[:, k * 256 : (k + 1) * 256], g, preferred_element_type=jnp.float32)
                total = part if total is None else total + part
            squares_ref[i, :, n * 256 : (n + 1) * 256] = total.astype(jnp.bfloat16)
    for i in range(HALF):
        cols = columns[i]
        cube = None
        for k in range(2):
            g = jnp.concatenate([store[table_ref[cols[0], cols[4 * k + b]]] for b in range(4)], axis=0)
            part = jnp.dot(
                squares_ref[i, :, k * 256 : (k + 1) * 256], g, preferred_element_type=jnp.float32
            )
            cube = part if cube is None else cube + part
        purified = 3.0 * squares_ref[i, :, 0:128].astype(jnp.float32) - 2.0 * cube
        out_ref[i, 0] = purified[:, :64].astype(jnp.bfloat16)


def vmem():
    return pl.BlockSpec(memory_space=pltpu.VMEM)


def half(far_half, table, center, other, halo, carried, rows_here):
    def out_block():
        core = lax.rem(lax.axis_index("rows"), 2)
        return ((1 - core) if far_half else core, 0, 0, 0)

    shape = jax.ShapeDtypeStruct((rows_here, 1, 64, 64), jnp.bfloat16)
    extra = [] if carried is None else [carried]
    return pl.pallas_call(
        functools.partial(half_kernel, far_half),
        grid=(1,),
        out_shape=shape,
        in_specs=[vmem()] * 4
        + [pl.BlockSpec(memory_space=pl.ANY)] * len(extra),
        out_specs=pl.BlockSpec((HALF, 1, 64, 64), lambda _: out_block()),
        scratch_shapes=[
            pltpu.VMEM((ZERO_TILE + 8, 64, 128), jnp.bfloat16),
            pltpu.SMEM((TABLE_ROWS + 8, 128), jnp.int32),
            pltpu.VMEM((HALF, 64, 512), jnp.bfloat16),
            pltpu.SemaphoreType.DMA,
        ],
        input_output_aliases={4: 0} if extra else {},
        compiler_params=pltpu.CompilerParams(vmem_limit_bytes=32 * 1024 * 1024),
        cost_estimate=pl.CostEstimate(flops=0, bytes_accessed=0, transcendentals=0),
        name="far_half" if far_half else "near_half",
    )(table, center, other, halo, *extra)


def local(block_values, pattern_cols, pattern_counts):
    rows_here = block_values.shape[0]
    count = lax.axis_size("rows")
    to_core = [(i, i ^ 1) for i in range(count)]
    to_chip = [(i, (i + 1 if i % 2 else i - 1) % count) for i in range(count)]
    packed = [jax.ShapeDtypeStruct((HALF * 4 * TILE + pad, 128), jnp.bfloat16) for pad in (PAD, 0)]
    block_values = pltpu.with_memory_space_constraint(block_values, pltpu.HBM)
    hbm = pl.BlockSpec(memory_space=pltpu.HBM)
    scratch = [pltpu.VMEM((HALF, 8, 64, 64), jnp.bfloat16), pltpu.SemaphoreType.DMA((HALF,))]
    free = pl.CostEstimate(flops=0, bytes_accessed=0, transcendentals=0)
    params = pltpu.CompilerParams(vmem_limit_bytes=32 * 1024 * 1024)
    near = pl.pallas_call(
        near_kernel,
        out_shape=packed[0],
        in_specs=[hbm],
        out_specs=vmem(),
        scratch_shapes=scratch,
        compiler_params=params,
        cost_estimate=free,
        name="pack_near",
    )(block_values)
    near_halo = lax.ppermute(near, "rows", to_chip)
    far, table = pl.pallas_call(
        far_kernel,
        out_shape=(packed[1], jax.ShapeDtypeStruct((TABLE_ROWS + 8, 128), jnp.int32)),
        in_specs=[hbm, vmem(), vmem(), pl.BlockSpec(memory_space=pl.ANY)],
        out_specs=(vmem(), vmem()),
        scratch_shapes=scratch,
        compiler_params=params,
        cost_estimate=free,
        name="pack_far",
    )(block_values, pattern_cols.T, pattern_counts.reshape(-1, 128), near)
    far_halo = lax.ppermute(far, "rows", to_core)
    result = half(True, table, far, near, far_halo, None, rows_here)
    return half(False, table, near, far, near_halo, result, rows_here)


def solution(mesh):
    in_specs = (P("rows", None, None, None), P(), P())
    out_specs = P("rows", "rep", None, None)
    return jax.shard_map(local, mesh=mesh, in_specs=in_specs, out_specs=out_specs, check_vma=False)
```

```python
import functools

import jax
import jax.numpy as jnp
from jax import lax
from jax.experimental import pallas as pl
from jax.experimental.pallas import tpu as pltpu
from jax.sharding import PartitionSpec as P

HALF = 8
PIECE = 4
WINDOW = 32
ZERO_TILE = WINDOW * 8
TABLE_ROWS = WINDOW + 8
TILE = 64
PAD = 16


def swapped(tile):
    return pltpu.roll(tile, 64, 1)


def pack_kernel(x_ref, near_ref, far_ref, rows, sems):
    core = lax.rem(lax.axis_index("rows"), 2)
    starts = (core * HALF, core * HALF + PIECE, (1 - core) * HALF, (1 - core) * HALF + PIECE)
    copies = [
        pltpu.make_async_copy(x_ref.at[pl.ds(start, PIECE)], rows.at[pl.ds(n * PIECE, PIECE)], sems.at[n])
        for n, start in enumerate(starts)
    ]
    for copy in copies:
        copy.start()
    near_ref[HALF * 4 * TILE :, :] = jnp.zeros((PAD, 128), jnp.bfloat16)
    for n, copy in enumerate(copies):
        copy.wait()
        out_ref = far_ref if n // 2 else near_ref
        for row in range(PIECE):
            for pair in range(4):
                at = pl.ds((((n % 2) * PIECE + row) * 4 + pair) * TILE, TILE)
                blocks = [rows[n * PIECE + row, 2 * pair + side] for side in range(2)]
                out_ref[at, :] = jnp.concatenate(blocks, axis=1)


def table_kernel(cols_ref, counts_ref, out_ref):
    total = cols_ref.shape[1]
    chunks = total // 128
    start = lax.rem(lax.axis_index("rows") * (2 * HALF) + (total - HALF), total)
    first = lax.div(start, 128)
    second = lax.rem(first + 1, chunks)
    offset = lax.rem(start, 128)
    shift = lax.rem(256 - offset, 256)

    def window(get):
        both = jnp.concatenate([get(first), get(second)], axis=1)
        return pltpu.roll(both, shift, 1)[:, :128]

    cols = window(lambda k: cols_ref[:, pl.ds(pl.multiple_of(k * 128, 128), 128)])
    counts = window(lambda k: jnp.broadcast_to(counts_ref[pl.ds(k, 1), :], (8, 128)))
    relative = cols - start
    relative = jnp.where(relative < 0, relative + total, relative)
    slot = lax.broadcasted_iota(jnp.int32, (8, 128), 0)
    lane = lax.broadcasted_iota(jnp.int32, (8, 128), 1)
    live = (slot < counts) & (lane < WINDOW)
    matchable = jnp.where(live & (relative < WINDOW), relative, -1)
    column = lax.broadcasted_iota(jnp.int32, (TABLE_ROWS, 128), 0)
    row = lax.broadcasted_iota(jnp.int32, (TABLE_ROWS, 128), 1)
    tiles = jnp.full((TABLE_ROWS, 128), ZERO_TILE, jnp.int32)
    for s in range(8):
        here = jnp.broadcast_to(matchable[s : s + 1, :], (TABLE_ROWS, 128)) == column
        tiles = jnp.where(here, row * 8 + ((s % 2) * 4 + s // 2), tiles)
    out_ref[0:TABLE_ROWS, :] = tiles
    out_ref[TABLE_ROWS : TABLE_ROWS + 8, :] = jnp.where(live, relative, WINDOW)


def half_kernel(far_half, table_in, center_ref, other_ref, halo_ref, *refs):
    out_ref, store, table_ref, squares_ref, sem = refs[-5:]
    fetch = pltpu.make_async_copy(table_in, table_ref, sem)
    fetch.start()
    core = lax.rem(lax.axis_index("rows"), 2)
    mine = lax.axis_index("rep")
    low_halo = core if far_half else 1 - core
    center = 2 - low_halo
    swap = lax.rem(mine, 2)
    pair_of = lax.div(mine, 2)

    zeros = jnp.zeros((64, 128), jnp.bfloat16)
    store[ZERO_TILE] = zeros
    store[ZERO_TILE + 4] = zeros
    for ref, chunk in ((center_ref, center), (other_ref, 3 - center), (halo_ref, 3 * (1 - low_halo))):
        for row in range(HALF):
            base = (chunk * HALF + row) * 8
            for pair in range(4):
                tile = ref[pl.ds((row * 4 + pair) * TILE, TILE), :]
                store[base + pair] = tile
                store[base + 4 + pair] = swapped(tile)
    fetch.wait()

    left = lax.broadcasted_iota(jnp.int16, (64, 128), 1) < 64
    columns = [
        [table_ref[TABLE_ROWS + (mine ^ q), center * HALF + i] for q in range(8)] for i in range(HALF)
    ]
    for i in range(HALF):
        cols = columns[i]
        at = (center * HALF + i) * 8 + swap * 4
        x = jnp.concatenate([store[at + (pair_of ^ p)] for p in range(4)], axis=1)

        def tile(p, b):
            one = table_ref[cols[2 * p], cols[b]]
            two = table_ref[cols[2 * p + 1], cols[b]] ^ 4
            return jnp.where(left, store[one], store[two])

        for n in range(2):
            total = None
            for k in range(2):
                g = jnp.concatenate(
                    [
                        jnp.concatenate([tile(2 * n + j, 4 * k + b) for j in range(2)], axis=1)
                        for b in range(4)
                    ],
                    axis=0,
                )
                part = jnp.dot(x[:, k * 256 : (k + 1) * 256], g, preferred_element_type=jnp.float32)
                total = part if total is None else total + part
            squares_ref[i, :, n * 256 : (n + 1) * 256] = total.astype(jnp.bfloat16)
    for i in range(HALF):
        cols = columns[i]
        cube = None
        for k in range(2):
            g = jnp.concatenate([store[table_ref[cols[0], cols[4 * k + b]]] for b in range(4)], axis=0)
            part = jnp.dot(
                squares_ref[i, :, k * 256 : (k + 1) * 256], g, preferred_element_type=jnp.float32
            )
            cube = part if cube is None else cube + part
        purified = 3.0 * squares_ref[i, :, 0:128].astype(jnp.float32) - 2.0 * cube
        out_ref[i, 0] = purified[:, :64].astype(jnp.bfloat16)


def vmem():
    return pl.BlockSpec(memory_space=pltpu.VMEM)


def half(far_half, table, center, other, halo, carried, rows_here):
    def out_block():
        core = lax.rem(lax.axis_index("rows"), 2)
        return ((1 - core) if far_half else core, 0, 0, 0)

    shape = jax.ShapeDtypeStruct((rows_here, 1, 64, 64), jnp.bfloat16)
    extra = [] if carried is None else [carried]
    return pl.pallas_call(
        functools.partial(half_kernel, far_half),
        grid=(1,),
        out_shape=shape,
        in_specs=[vmem()] * 4
        + [pl.BlockSpec(memory_space=pl.ANY)] * len(extra),
        out_specs=pl.BlockSpec((HALF, 1, 64, 64), lambda _: out_block()),
        scratch_shapes=[
            pltpu.VMEM((ZERO_TILE + 8, 64, 128), jnp.bfloat16),
            pltpu.SMEM((TABLE_ROWS + 8, 128), jnp.int32),
            pltpu.VMEM((HALF, 64, 512), jnp.bfloat16),
            pltpu.SemaphoreType.DMA,
        ],
        input_output_aliases={4: 0} if extra else {},
        compiler_params=pltpu.CompilerParams(vmem_limit_bytes=32 * 1024 * 1024),
        cost_estimate=pl.CostEstimate(flops=0, bytes_accessed=0, transcendentals=0),
        name="far_half" if far_half else "near_half",
    )(table, center, other, halo, *extra)


def local(block_values, pattern_cols, pattern_counts):
    rows_here = block_values.shape[0]
    count = lax.axis_size("rows")
    to_core = [(i, i ^ 1) for i in range(count)]
    to_chip = [(i, (i + 1 if i % 2 else i - 1) % count) for i in range(count)]
    packed = [jax.ShapeDtypeStruct((HALF * 4 * TILE + pad, 128), jnp.bfloat16) for pad in (PAD, 0)]
    block_values = pltpu.with_memory_space_constraint(block_values, pltpu.HBM)
    free = pl.CostEstimate(flops=0, bytes_accessed=0, transcendentals=0)
    near, far = pl.pallas_call(
        pack_kernel,
        out_shape=packed,
        in_specs=[pl.BlockSpec(memory_space=pltpu.HBM)],
        out_specs=[vmem(), vmem()],
        scratch_shapes=[
            pltpu.VMEM((2 * HALF, 8, 64, 64), jnp.bfloat16),
            pltpu.SemaphoreType.DMA((2 * HALF // PIECE,)),
        ],
        compiler_params=pltpu.CompilerParams(vmem_limit_bytes=32 * 1024 * 1024),
        cost_estimate=free,
        name="pack",
    )(block_values)
    near_halo = lax.ppermute(near, "rows", to_chip)
    far_halo = lax.ppermute(far, "rows", to_core)
    table = pl.pallas_call(
        table_kernel,
        out_shape=jax.ShapeDtypeStruct((TABLE_ROWS + 8, 128), jnp.int32),
        in_specs=[vmem(), vmem()],
        out_specs=vmem(),
        cost_estimate=free,
        name="table",
    )(pattern_cols.T, pattern_counts.reshape(-1, 128))
    result = half(True, table, far, near, far_halo, None, rows_here)
    return half(False, table, near, far, near_halo, result, rows_here)


def solution(mesh):
    in_specs = (P("rows", None, None, None), P(), P())
    out_specs = P("rows", "rep", None, None)
    return jax.shard_map(local, mesh=mesh, in_specs=in_specs, out_specs=out_specs, check_vma=False)
```

```python
import jax
import jax.numpy as jnp
from jax import lax
from jax.experimental import pallas as pl
from jax.experimental.pallas import tpu as pltpu
from jax.sharding import PartitionSpec as P

HALF = 8
PIECE = 4
WINDOW = 32
TILE = 64
PAD = 16
GROUP = 12
ZERO_TILE = WINDOW * GROUP
STORE = (ZERO_TILE + 8, TILE, 128)
STRIDE = 64
TABLE = (24, 128)
COLUMNS = WINDOW * STRIDE + STRIDE


def fill(store, chunk, ref):
    for row in range(HALF):
        base = (chunk * HALF + row) * GROUP
        for pair in range(4):
            tile = ref[pl.ds((row * 4 + pair) * TILE, TILE), :]
            store[base + pair] = tile
            store[base + 4 + pair] = pltpu.roll(tile, 64, 1)
            store[base + 8 + pair] = tile


def pack_kernel(x_ref, near_ref, far_ref, rows, sems):
    core = lax.rem(lax.axis_index("rows"), 2)
    starts = (core * HALF, core * HALF + PIECE, (1 - core) * HALF, (1 - core) * HALF + PIECE)
    copies = [
        pltpu.make_async_copy(x_ref.at[pl.ds(start, PIECE)], rows.at[pl.ds(n * PIECE, PIECE)], sems.at[n])
        for n, start in enumerate(starts)
    ]
    for copy in copies:
        copy.start()
    near_ref[HALF * 4 * TILE :, :] = jnp.zeros((PAD, 128), jnp.bfloat16)
    for n, copy in enumerate(copies):
        copy.wait()
        out_ref = far_ref if n // 2 else near_ref
        for row in range(PIECE):
            for pair in range(4):
                at = pl.ds((((n % 2) * PIECE + row) * 4 + pair) * TILE, TILE)
                blocks = [rows[n * PIECE + row, 2 * pair + side] for side in range(2)]
                out_ref[at, :] = jnp.concatenate(blocks, axis=1)


def own_kernel(near_ref, far_ref, cols_in, counts_in, table_ref, store, cols_ref, counts_ref, sems):
    copies = [
        pltpu.make_async_copy(cols_in, cols_ref, sems.at[0]),
        pltpu.make_async_copy(counts_in, counts_ref, sems.at[1]),
    ]
    for copy in copies:
        copy.start()
    core = lax.rem(lax.axis_index("rows"), 2)
    zeros = jnp.zeros((TILE, 128), jnp.bfloat16)
    store[ZERO_TILE] = zeros
    store[ZERO_TILE + 4] = zeros
    fill(store, 1 + core, near_ref)
    fill(store, 2 - core, far_ref)
    for copy in copies:
        copy.wait()
    total = cols_ref.shape[1]
    chunks = total // 128
    start = lax.rem(lax.axis_index("rows") * (2 * HALF) + (total - HALF), total)
    first = lax.div(start, 128)
    second = lax.rem(first + 1, chunks)
    shift = lax.rem(256 - lax.rem(start, 128), 256)

    def window(get):
        both = jnp.concatenate([get(first), get(second)], axis=1)
        return pltpu.roll(both, shift, 1)[:, :128]

    cols = window(lambda k: cols_ref[:, pl.ds(pl.multiple_of(k * 128, 128), 128)])
    counts = window(lambda k: jnp.broadcast_to(counts_ref[pl.ds(k, 1), :], (8, 128)))
    relative = cols - start
    relative = jnp.where(relative < 0, relative + total, relative)
    slot = lax.broadcasted_iota(jnp.int32, (8, 128), 0)
    lane = lax.broadcasted_iota(jnp.int32, (8, 128), 1)
    live = (slot < counts) & (lane < WINDOW)
    matchable = jnp.where(live & (relative < WINDOW), relative, -1)
    matchable = jnp.where(lane < STRIDE, matchable, pltpu.roll(matchable, STRIDE, 1))
    line = lax.broadcasted_iota(jnp.int32, (16, 128), 0)
    lane = lax.broadcasted_iota(jnp.int32, (16, 128), 1)
    column = line * 2 + lane // STRIDE
    row = lane % STRIDE
    tiles = jnp.full((16, 128), ZERO_TILE, jnp.int32)
    for s in range(8):
        here = jnp.broadcast_to(matchable[s : s + 1, :], (16, 128)) == column
        tiles = jnp.where(here, row * GROUP + ((s % 2) * 4 + s // 2), tiles)
    table_ref[0:16, :] = tiles
    columns = pltpu.roll(jnp.where(live, relative, WINDOW), STRIDE, 1)
    table_ref[16:24, :] = jnp.where(lane[0:8, :] < STRIDE, ZERO_TILE, columns)


def purify(table_in, halo_ref, store, table_ref, squares_ref, sem, center, halo_chunk, put):
    fetch = pltpu.make_async_copy(table_in, table_ref, sem)
    fetch.start()
    mine = lax.axis_index("rep")
    swap = lax.rem(mine, 2)
    pair_of = lax.div(mine, 2)
    fill(store, halo_chunk, halo_ref)
    left = lax.broadcasted_iota(jnp.int16, (TILE, 128), 1) < 64
    fetch.wait()
    rows = [
        [table_ref[COLUMNS + (mine ^ q) * 128 + center * HALF + i] for q in range(8)]
        for i in range(HALF)
    ]
    for i in range(HALF):
        cols = [c * STRIDE for c in rows[i]]
        at = (center * HALF + i) * GROUP + swap * 4
        x = jnp.concatenate([store[at + (pair_of ^ p)] for p in range(4)], axis=1)

        def tile(p, b):
            one = table_ref[cols[2 * p] + rows[i][b]]
            two = table_ref[cols[2 * p + 1] + rows[i][b]]
            return jnp.where(left, store[one], store[two + 4])

        for n in range(2):
            total = None
            for k in range(2):
                g = jnp.concatenate(
                    [
                        jnp.concatenate([tile(2 * n + j, 4 * k + b) for j in range(2)], axis=1)
                        for b in range(4)
                    ],
                    axis=0,
                )
                part = jnp.dot(x[:, k * 256 : (k + 1) * 256], g, preferred_element_type=jnp.float32)
                total = part if total is None else total + part
            squares_ref[i, :, n * 256 : (n + 1) * 256] = total.astype(jnp.bfloat16)
    for i in range(HALF):
        column = rows[i][0] * STRIDE
        cube = None
        for k in range(2):
            g = jnp.concatenate([store[table_ref[column + rows[i][4 * k + b]]] for b in range(4)], axis=0)
            part = jnp.dot(
                squares_ref[i, :, k * 256 : (k + 1) * 256], g, preferred_element_type=jnp.float32
            )
            cube = part if cube is None else cube + part
        purified = 3.0 * squares_ref[i, :, 0:128].astype(jnp.float32) - 2.0 * cube
        put(i, purified[:, :64].astype(jnp.bfloat16))


def far_kernel(table_in, halo_ref, _, out_ref, store, table_ref, squares_ref, sem):
    core = lax.rem(lax.axis_index("rows"), 2)

    def put(i, block):
        out_ref[i] = block

    purify(table_in, halo_ref, store, table_ref, squares_ref, sem, 2 - core, 3 * (1 - core), put)


def near_kernel(table_in, halo_ref, far_ref, _, out_ref, store, table_ref, squares_ref, sem, near, sems):
    core = lax.rem(lax.axis_index("rows"), 2)
    far_out = pltpu.make_async_copy(far_ref, out_ref.at[pl.ds((1 - core) * HALF, HALF), 0], sems.at[0])
    far_out.start()

    def put(i, block):
        near[i] = block

    purify(table_in, halo_ref, store, table_ref, squares_ref, sem, 1 + core, 3 * core, put)
    near_out = pltpu.make_async_copy(near, out_ref.at[pl.ds(core * HALF, HALF), 0], sems.at[1])
    near_out.start()
    far_out.wait()
    near_out.wait()


def vmem():
    return pl.BlockSpec(memory_space=pltpu.VMEM)


def hbm():
    return pl.BlockSpec(memory_space=pltpu.HBM)


def call(kernel, name, args, in_specs, out_shape, out_specs, scratch_shapes=(), aliases=None):
    return pl.pallas_call(
        kernel,
        out_shape=out_shape,
        in_specs=in_specs,
        out_specs=out_specs,
        scratch_shapes=scratch_shapes,
        input_output_aliases=aliases or {},
        compiler_params=pltpu.CompilerParams(vmem_limit_bytes=16 * 1024 * 1024),
        cost_estimate=pl.CostEstimate(flops=0, bytes_accessed=0, transcendentals=0),
        name=name,
    )(*args)


def local(block_values, pattern_cols, pattern_counts):
    count = lax.axis_size("rows")
    to_core = [(i, i ^ 1) for i in range(count)]
    to_chip = [(i, (i + 1 if i % 2 else i - 1) % count) for i in range(count)]
    bf16, i32 = jnp.bfloat16, jnp.int32
    near, far = call(
        pack_kernel,
        "pack",
        [pltpu.with_memory_space_constraint(block_values, pltpu.HBM)],
        [hbm()],
        [jax.ShapeDtypeStruct((HALF * 4 * TILE + pad, 128), bf16) for pad in (PAD, 0)],
        [vmem(), vmem()],
        [
            pltpu.VMEM((2 * HALF, 8, 64, 64), bf16),
            pltpu.SemaphoreType.DMA((2 * HALF // PIECE,)),
        ],
    )
    near_halo = lax.ppermute(near, "rows", to_chip)
    far_halo = lax.ppermute(far, "rows", to_core)
    cols, counts = pattern_cols.T, pattern_counts.reshape(-1, 128)
    stored = jax.ShapeDtypeStruct(STORE, bf16)
    table, store = call(
        own_kernel,
        "own",
        [near, far, *(pltpu.with_memory_space_constraint(x, pltpu.HBM) for x in (cols, counts))],
        [vmem(), vmem(), hbm(), hbm()],
        [jax.ShapeDtypeStruct(TABLE, i32), stored],
        [vmem(), vmem()],
        [
            pltpu.VMEM(cols.shape, i32),
            pltpu.VMEM(counts.shape, i32),
            pltpu.SemaphoreType.DMA((2,)),
        ],
    )
    table = table.reshape(-1)
    scratch = [
        pltpu.SMEM((TABLE[0] * TABLE[1],), i32),
        pltpu.VMEM((HALF, 64, 512), bf16),
        pltpu.SemaphoreType.DMA,
    ]
    far_result, store = call(
        far_kernel,
        "far_half",
        [table, far_halo, store],
        [vmem()] * 3,
        [jax.ShapeDtypeStruct((HALF, 64, 64), bf16), stored],
        [vmem(), vmem()],
        scratch,
        {2: 1},
    )
    result, _ = call(
        near_kernel,
        "near_half",
        [table, near_halo, far_result, store],
        [vmem()] * 4,
        [jax.ShapeDtypeStruct((2 * HALF, 1, 64, 64), bf16), stored],
        [hbm(), vmem()],
        scratch + [pltpu.VMEM((HALF, 64, 64), bf16), pltpu.SemaphoreType.DMA((2,))],
        {3: 1},
    )
    return result


def solution(mesh):
    in_specs = (P("rows", None, None, None), P(), P())
    out_specs = P("rows", "rep", None, None)
    return jax.shard_map(local, mesh=mesh, in_specs=in_specs, out_specs=out_specs, check_vma=False)
```

```python
import jax
import jax.numpy as jnp
from jax import lax
from jax.experimental import pallas as pl
from jax.experimental.pallas import tpu as pltpu
from jax.sharding import PartitionSpec as P

HALF = 8
PIECE = 4
WINDOW = 32
TILE = 64
PAD = 16
GROUP = 12
ZERO_TILE = WINDOW * GROUP
STORE = (ZERO_TILE + 8, TILE, 128)
STRIDE = 64
TABLE = (24, 128)
COLUMNS = WINDOW * STRIDE + STRIDE


def fill(store, chunk, ref):
    for row in range(HALF):
        base = (chunk * HALF + row) * GROUP
        for pair in range(4):
            tile = ref[pl.ds((row * 4 + pair) * TILE, TILE), :]
            store[base + pair] = tile
            store[base + 4 + pair] = pltpu.roll(tile, 64, 1)
            store[base + 8 + pair] = tile


def from_pieces(x_ref, rows, sems, starts):
    return [
        pltpu.make_async_copy(x_ref.at[pl.ds(start, PIECE)], rows.at[pl.ds(n * PIECE, PIECE)], sems.at[n])
        for n, start in enumerate(starts)
    ]


def pack(copies, rows, out_ref):
    for n, copy in enumerate(copies):
        copy.wait()
        for row in range(n * PIECE, (n + 1) * PIECE):
            for pair in range(4):
                at = pl.ds((row * 4 + pair) * TILE, TILE)
                blocks = [rows[row, 2 * pair + side] for side in range(2)]
                out_ref[at, :] = jnp.concatenate(blocks, axis=1)


def pack_kernel(x_ref, near_ref, far_ref, near_rows, far_rows, near_sems, far_sems):
    me = lax.axis_index("rows")
    core = lax.rem(me, 2)
    late = me == lax.axis_size("rows") - 1
    near = from_pieces(x_ref, near_rows, near_sems, (core * HALF, core * HALF + PIECE))
    far = from_pieces(x_ref, far_rows, far_sems, ((1 - core) * HALF, (1 - core) * HALF + PIECE))
    for copy in near:
        copy.start()

    @pl.when(jnp.logical_not(late))
    def _():
        for copy in far:
            copy.start()

    near_ref[HALF * 4 * TILE :, :] = jnp.zeros((PAD, 128), jnp.bfloat16)
    pack(near, near_rows, near_ref)

    @pl.when(jnp.logical_not(late))
    def _():
        pack(far, far_rows, far_ref)


def rest_kernel(x_ref, _, far_ref, far_rows, far_sems):
    me = lax.axis_index("rows")
    core = lax.rem(me, 2)

    @pl.when(me == lax.axis_size("rows") - 1)
    def _():
        far = from_pieces(x_ref, far_rows, far_sems, ((1 - core) * HALF, (1 - core) * HALF + PIECE))
        for copy in far:
            copy.start()
        pack(far, far_rows, far_ref)


def own_kernel(near_ref, far_ref, cols_in, counts_in, table_ref, store, cols_ref, counts_ref, sems):
    copies = [
        pltpu.make_async_copy(cols_in, cols_ref, sems.at[0]),
        pltpu.make_async_copy(counts_in, counts_ref, sems.at[1]),
    ]
    for copy in copies:
        copy.start()
    core = lax.rem(lax.axis_index("rows"), 2)
    zeros = jnp.zeros((TILE, 128), jnp.bfloat16)
    store[ZERO_TILE] = zeros
    store[ZERO_TILE + 4] = zeros
    fill(store, 1 + core, near_ref)
    fill(store, 2 - core, far_ref)
    for copy in copies:
        copy.wait()
    total = cols_ref.shape[1]
    chunks = total // 128
    start = lax.rem(lax.axis_index("rows") * (2 * HALF) + (total - HALF), total)
    first = lax.div(start, 128)
    second = lax.rem(first + 1, chunks)
    shift = lax.rem(256 - lax.rem(start, 128), 256)

    def window(get):
        both = jnp.concatenate([get(first), get(second)], axis=1)
        return pltpu.roll(both, shift, 1)[:, :128]

    cols = window(lambda k: cols_ref[:, pl.ds(pl.multiple_of(k * 128, 128), 128)])
    counts = window(lambda k: jnp.broadcast_to(counts_ref[pl.ds(k, 1), :], (8, 128)))
    relative = cols - start
    relative = jnp.where(relative < 0, relative + total, relative)
    slot = lax.broadcasted_iota(jnp.int32, (8, 128), 0)
    lane = lax.broadcasted_iota(jnp.int32, (8, 128), 1)
    live = (slot < counts) & (lane < WINDOW)
    matchable = jnp.where(live & (relative < WINDOW), relative, -1)
    matchable = jnp.where(lane < STRIDE, matchable, pltpu.roll(matchable, STRIDE, 1))
    line = lax.broadcasted_iota(jnp.int32, (16, 128), 0)
    lane = lax.broadcasted_iota(jnp.int32, (16, 128), 1)
    column = line * 2 + lane // STRIDE
    row = lane % STRIDE
    tiles = jnp.full((16, 128), ZERO_TILE, jnp.int32)
    for s in range(8):
        here = jnp.broadcast_to(matchable[s : s + 1, :], (16, 128)) == column
        tiles = jnp.where(here, row * GROUP + ((s % 2) * 4 + s // 2), tiles)
    table_ref[0:16, :] = tiles
    columns = pltpu.roll(jnp.where(live, relative, WINDOW), STRIDE, 1)
    table_ref[16:24, :] = jnp.where(lane[0:8, :] < STRIDE, ZERO_TILE, columns)


def purify(table_ref, store, squares_ref, center, put):
    mine = lax.axis_index("rep")
    swap = lax.rem(mine, 2)
    pair_of = lax.div(mine, 2)
    left = lax.broadcasted_iota(jnp.int16, (TILE, 128), 1) < 64
    rows = [
        [table_ref[COLUMNS + (mine ^ q) * 128 + center * HALF + i] for q in range(8)]
        for i in range(HALF)
    ]
    for i in range(HALF):
        cols = [c * STRIDE for c in rows[i]]
        at = (center * HALF + i) * GROUP + swap * 4
        x = jnp.concatenate([store[at + (pair_of ^ p)] for p in range(4)], axis=1)

        def tile(p, b):
            one = table_ref[cols[2 * p] + rows[i][b]]
            two = table_ref[cols[2 * p + 1] + rows[i][b]]
            return jnp.where(left, store[one], store[two + 4])

        for n in range(2):
            total = None
            for k in range(2):
                g = jnp.concatenate(
                    [
                        jnp.concatenate([tile(2 * n + j, 4 * k + b) for j in range(2)], axis=1)
                        for b in range(4)
                    ],
                    axis=0,
                )
                part = jnp.dot(x[:, k * 256 : (k + 1) * 256], g, preferred_element_type=jnp.float32)
                total = part if total is None else total + part
            squares_ref[i, :, n * 256 : (n + 1) * 256] = total.astype(jnp.bfloat16)
    for i in range(HALF):
        column = rows[i][0] * STRIDE
        cube = None
        for k in range(2):
            g = jnp.concatenate([store[table_ref[column + rows[i][4 * k + b]]] for b in range(4)], axis=0)
            part = jnp.dot(
                squares_ref[i, :, k * 256 : (k + 1) * 256], g, preferred_element_type=jnp.float32
            )
            cube = part if cube is None else cube + part
        purified = 3.0 * squares_ref[i, :, 0:128].astype(jnp.float32) - 2.0 * cube
        put(i, purified[:, :64].astype(jnp.bfloat16))


def far_kernel(table_in, halo_ref, _, out_ref, store, table_ref, squares_ref, sem):
    me = lax.axis_index("rows")
    core = lax.rem(me, 2)
    fetch = pltpu.make_async_copy(table_in, table_ref, sem)
    fetch.start()
    fill(store, 3 * (1 - core), halo_ref)
    fetch.wait()

    def put(i, block):
        out_ref[i] = block

    @pl.when(me != 1)
    def _():
        purify(table_ref, store, squares_ref, 2 - core, put)


def near_kernel(
    table_in, halo_ref, far_in, _, out_ref, store, table_ref, squares_ref, sem, near, far, sems
):
    me = lax.axis_index("rows")
    core = lax.rem(me, 2)
    fetch = pltpu.make_async_copy(table_in, table_ref, sem)
    fetch.start()
    near_out = pltpu.make_async_copy(near, out_ref.at[pl.ds(core * HALF, HALF), 0], sems.at[0])
    far_at = out_ref.at[pl.ds((1 - core) * HALF, HALF), 0]
    far_out = pltpu.make_async_copy(far_in, far_at, sems.at[1])

    @pl.when(me != 1)
    def _():
        far_out.start()

    fill(store, 3 * core, halo_ref)
    fetch.wait()

    def put(i, block):
        near[i] = block

    purify(table_ref, store, squares_ref, 1 + core, put)
    near_out.start()

    @pl.when(me == 1)
    def _():
        def put_far(i, block):
            far[i] = block

        purify(table_ref, store, squares_ref, 2 - core, put_far)
        late_out = pltpu.make_async_copy(far, far_at, sems.at[1])
        late_out.start()
        late_out.wait()

    @pl.when(me != 1)
    def _():
        far_out.wait()

    near_out.wait()


def vmem():
    return pl.BlockSpec(memory_space=pltpu.VMEM)


def hbm():
    return pl.BlockSpec(memory_space=pltpu.HBM)


def call(kernel, name, args, in_specs, out_shape, out_specs, scratch_shapes=(), aliases=None):
    return pl.pallas_call(
        kernel,
        out_shape=out_shape,
        in_specs=in_specs,
        out_specs=out_specs,
        scratch_shapes=scratch_shapes,
        input_output_aliases=aliases or {},
        compiler_params=pltpu.CompilerParams(vmem_limit_bytes=16 * 1024 * 1024),
        cost_estimate=pl.CostEstimate(flops=0, bytes_accessed=0, transcendentals=0),
        name=name,
    )(*args)


def local(block_values, pattern_cols, pattern_counts):
    count = lax.axis_size("rows")
    to_core = [(i, i ^ 1) for i in range(count)]
    to_chip = [(i, (i + 1 if i % 2 else i - 1) % count) for i in range(count)]
    bf16, i32 = jnp.bfloat16, jnp.int32
    block_values = pltpu.with_memory_space_constraint(block_values, pltpu.HBM)
    rows = [pltpu.VMEM((HALF, 8, 64, 64), bf16)]
    sems = [pltpu.SemaphoreType.DMA((HALF // PIECE,))]
    packed = [jax.ShapeDtypeStruct((HALF * 4 * TILE + pad, 128), bf16) for pad in (PAD, 0)]
    near, far = call(
        pack_kernel, "pack", [block_values], [hbm()], packed, [vmem(), vmem()], rows * 2 + sems * 2
    )
    far = call(
        rest_kernel,
        "rest",
        [block_values, far],
        [hbm(), vmem()],
        packed[1],
        vmem(),
        rows + sems,
        {1: 0},
    )
    near_halo = lax.ppermute(near, "rows", to_chip)
    far_halo = lax.ppermute(far, "rows", to_core)
    cols, counts = pattern_cols.T, pattern_counts.reshape(-1, 128)
    stored = jax.ShapeDtypeStruct(STORE, bf16)
    table, store = call(
        own_kernel,
        "own",
        [near, far, *(pltpu.with_memory_space_constraint(x, pltpu.HBM) for x in (cols, counts))],
        [vmem(), vmem(), hbm(), hbm()],
        [jax.ShapeDtypeStruct(TABLE, i32), stored],
        [vmem(), vmem()],
        [
            pltpu.VMEM(cols.shape, i32),
            pltpu.VMEM(counts.shape, i32),
            pltpu.SemaphoreType.DMA((2,)),
        ],
    )
    table = table.reshape(-1)
    scratch = [
        pltpu.SMEM((TABLE[0] * TABLE[1],), i32),
        pltpu.VMEM((HALF, 64, 512), bf16),
        pltpu.SemaphoreType.DMA,
    ]
    far_result, store = call(
        far_kernel,
        "far_half",
        [table, far_halo, store],
        [vmem()] * 3,
        [jax.ShapeDtypeStruct((HALF, 64, 64), bf16), stored],
        [vmem(), vmem()],
        scratch,
        {2: 1},
    )
    result, _ = call(
        near_kernel,
        "near_half",
        [table, near_halo, far_result, store],
        [vmem()] * 4,
        [jax.ShapeDtypeStruct((2 * HALF, 1, 64, 64), bf16), stored],
        [hbm(), vmem()],
        scratch + [pltpu.VMEM((HALF, 64, 64), bf16)] * 2 + [pltpu.SemaphoreType.DMA((2,))],
        {3: 1},
    )
    return result


def solution(mesh):
    in_specs = (P("rows", None, None, None), P(), P())
    out_specs = P("rows", "rep", None, None)
    return jax.shard_map(local, mesh=mesh, in_specs=in_specs, out_specs=out_specs, check_vma=False)
```

```python
import functools

import jax
import jax.numpy as jnp
from jax import lax
from jax.experimental import pallas as pl
from jax.experimental.pallas import tpu as pltpu
from jax.sharding import PartitionSpec as P

HALF = 8
PIECE = 4
WINDOW = 32
TILE = 64
PAD = 16
GROUP = 12
ZERO_TILE = WINDOW * GROUP
STORE = (ZERO_TILE + 8, TILE, 128)
TABLES = (2, 8, 128)
DEAD = (WINDOW - 1, 0)
COLUMN_LINE = (6, 1)


def fill(store, chunk, ref):
    for row in range(HALF):
        base = (chunk * HALF + row) * GROUP
        for pair in range(4):
            tile = ref[pl.ds((row * 4 + pair) * TILE, TILE), :]
            store[base + pair] = tile
            store[base + 4 + pair] = pltpu.roll(tile, 64, 1)
            store[base + 8 + pair] = tile


def from_pieces(x_ref, rows, sems, starts):
    return [
        pltpu.make_async_copy(x_ref.at[pl.ds(start, PIECE)], rows.at[pl.ds(n * PIECE, PIECE)], sems.at[n])
        for n, start in enumerate(starts)
    ]


def pack(copies, rows, out_ref):
    for n, copy in enumerate(copies):
        copy.wait()
        for row in range(n * PIECE, (n + 1) * PIECE):
            for pair in range(4):
                at = pl.ds((row * 4 + pair) * TILE, TILE)
                blocks = [rows[row, 2 * pair + side] for side in range(2)]
                out_ref[at, :] = jnp.concatenate(blocks, axis=1)


def rest_kernel(x_ref, _, far_ref, far_rows, far_sems):
    me = lax.axis_index("rows")
    core = lax.rem(me, 2)

    @pl.when(me == lax.axis_size("rows") - 1)
    def _():
        far = from_pieces(x_ref, far_rows, far_sems, ((1 - core) * HALF, (1 - core) * HALF + PIECE))
        for copy in far:
            copy.start()
        pack(far, far_rows, far_ref)


def own(near_ref, far_ref, cols_in, counts_in, table_ref, store, cols_ref, counts_ref, sems):
    copies = [
        pltpu.make_async_copy(cols_in, cols_ref, sems.at[0]),
        pltpu.make_async_copy(counts_in, counts_ref, sems.at[1]),
    ]
    for copy in copies:
        copy.start()
    core = lax.rem(lax.axis_index("rows"), 2)
    zeros = jnp.zeros((TILE, 128), jnp.bfloat16)
    store[ZERO_TILE] = zeros
    store[ZERO_TILE + 4] = zeros
    fill(store, 1 + core, near_ref)
    fill(store, 2 - core, far_ref)
    for copy in copies:
        copy.wait()
    total = cols_ref.shape[1]
    chunks = total // 128
    start = lax.rem(lax.axis_index("rows") * (2 * HALF) + (total - HALF), total)
    first = lax.div(start, 128)
    second = lax.rem(first + 1, chunks)
    shift = lax.rem(256 - lax.rem(start, 128), 256)

    def window(get):
        both = jnp.concatenate([get(first), get(second)], axis=1)
        return pltpu.roll(both, shift, 1)[:, :128]

    cols = window(lambda k: cols_ref[:, pl.ds(pl.multiple_of(k * 128, 128), 128)])
    counts = window(lambda k: jnp.broadcast_to(counts_ref[pl.ds(k, 1), :], (8, 128)))
    relative = cols - start
    relative = jnp.where(relative < 0, relative + total, relative)
    slot = lax.broadcasted_iota(jnp.int32, (8, 128), 0)
    lane = lax.broadcasted_iota(jnp.int32, (8, 128), 1)
    live = (slot < counts) & (lane < WINDOW)
    matchable = jnp.where(live & (relative < WINDOW), relative, -1)
    matchable = functools.reduce(
        jnp.maximum, [matchable] + [pltpu.roll(matchable, by, 1) for by in (32, 64, 96)]
    )
    column = slot * 4 + lane // WINDOW
    row = lane % WINDOW
    tiles = jnp.full((8, 128), ZERO_TILE, jnp.int32)
    for s in range(8):
        here = jnp.broadcast_to(matchable[s : s + 1, :], (8, 128)) == column
        tiles = jnp.where(here, row * GROUP + ((s % 2) * 4 + s // 2), tiles)
    reached = ((column < 24) & (row < 24), (column >= 8) & (row >= 8))
    for high in range(2):
        columns = jnp.where(live, relative, DEAD[high])
        line = jnp.zeros((8, 128), jnp.int32)
        for s in range(8):
            moved = pltpu.roll(columns, (s * 8 - HALF * (1 + high)) % 128, 1)
            line = jnp.where(lane // 8 == s, jnp.broadcast_to(moved[s : s + 1, :], (8, 128)), line)
        words = jnp.where(reached[high], tiles, ZERO_TILE)
        table_ref[high] = jnp.where(slot == COLUMN_LINE[high], line, words)


def columns_of(word, center):
    mine = lax.axis_index("rep")
    start = jnp.where(center == 1, COLUMN_LINE[0], COLUMN_LINE[1]) * 128
    return [
        [word(start + (mine ^ q) * 8 + i) for q in range(8)] for i in range(HALF)
    ]


def left_side():
    return lax.broadcasted_iota(jnp.int16, (TILE, 128), 1) < 64


def gathered(word, store, left, cols, sources, n):
    def tile(p, source):
        one = word(cols[2 * p] * WINDOW + source)
        two = word(cols[2 * p + 1] * WINDOW + source)
        return jnp.where(left, store[one], store[two + 4])

    return jnp.concatenate(
        [jnp.concatenate([tile(2 * n + j, b) for j in range(2)], axis=1) for b in sources], axis=0
    )


def product(x, word, store, left, cols, sources, n):
    total = None
    for k in range(0, len(sources), 4):
        g = gathered(word, store, left, cols, sources[k : k + 4], n)
        part = jnp.dot(x[:, k * 64 : (k + 4) * 64], g, preferred_element_type=jnp.float32)
        total = part if total is None else total + part
    return total


def squares(word, store, center, rows, put, skip=None):
    mine = lax.axis_index("rep")
    left = left_side()
    for i in range(HALF):
        at = (center * HALF + i) * GROUP + lax.rem(mine, 2) * 4
        x = jnp.concatenate([store[at + (lax.div(mine, 2) ^ p)] for p in range(4)], axis=1)
        sources = rows[i]
        if skip is not None:
            sources = [jnp.where(lax.div(c, HALF) == skip, DEAD[0], c) for c in sources]
        for n in range(2):
            put(i, n, product(x, word, store, left, rows[i], sources, n))


def low_halo_squares(word, store, rows, put):
    left = left_side()
    for i in range(HALF):
        sources = list(range(i, HALF + i % 2))
        found = [word(w * WINDOW + HALF + i) if w < HALF else ZERO_TILE for w in sources]
        x = jnp.concatenate(
            [
                jnp.where(left, store[found[k]], store[found[k + 1] + 4])
                for k in range(0, len(sources), 2)
            ],
            axis=1,
        )
        for n in range(2):
            put(i, n, product(x, word, store, left, rows[i], sources, n))


def cubes(word, store, squares_ref, rows, put):
    for i in range(HALF):
        cube = None
        for k in range(2):
            g = jnp.concatenate(
                [store[word(rows[i][0] * WINDOW + c)] for c in rows[i][4 * k : 4 * k + 4]], axis=0
            )
            part = jnp.dot(
                squares_ref[i, :, k * 256 : (k + 1) * 256], g, preferred_element_type=jnp.float32
            )
            cube = part if cube is None else cube + part
        purified = 3.0 * squares_ref[i, :, 0:128].astype(jnp.float32) - 2.0 * cube
        put(i, purified[:, :64].astype(jnp.bfloat16))


def rounded(squares_ref, before=None):
    def put(i, n, total):
        at = slice(n * 256, (n + 1) * 256)
        if before is not None:
            total = total + before[i, :, at]
        squares_ref[i, :, at] = total.astype(jnp.bfloat16)

    return put


def pack_kernel(
    x_ref,
    cols_in,
    counts_in,
    near_ref,
    far_ref,
    tables_ref,
    store,
    early_ref,
    near_rows,
    far_rows,
    near_sems,
    far_sems,
    cols_ref,
    counts_ref,
    own_sems,
    table_ref,
    fetch_sem,
):
    me = lax.axis_index("rows")
    core = lax.rem(me, 2)
    late = me == lax.axis_size("rows") - 1
    near = from_pieces(x_ref, near_rows, near_sems, (core * HALF, core * HALF + PIECE))
    far = from_pieces(x_ref, far_rows, far_sems, ((1 - core) * HALF, (1 - core) * HALF + PIECE))
    for copy in near:
        copy.start()

    @pl.when(jnp.logical_not(late))
    def _():
        for copy in far:
            copy.start()

    near_ref[HALF * 4 * TILE :, :] = jnp.zeros((PAD, 128), jnp.bfloat16)
    pack(near, near_rows, near_ref)

    @pl.when(jnp.logical_not(late))
    def _():
        pack(far, far_rows, far_ref)

    @pl.when(me == 0)
    def _():
        own(near_ref, far_ref, cols_in, counts_in, tables_ref, store, cols_ref, counts_ref, own_sems)
        fetch = pltpu.make_async_copy(tables_ref.at[0], table_ref, fetch_sem)
        fetch.start()
        fetch.wait()

        def word(at):
            return table_ref[lax.div(at, 128), lax.rem(at, 128)]

        def put(i, n, total):
            early_ref[i, :, n * 256 : (n + 1) * 256] = total

        squares(word, store, 1, columns_of(word, 1), put, skip=0)


def own_kernel(near_ref, far_ref, cols_in, counts_in, _, __, tables_ref, store, cols_ref, counts_ref, sems):
    @pl.when(lax.axis_index("rows") != 0)
    def _():
        own(near_ref, far_ref, cols_in, counts_in, tables_ref, store, cols_ref, counts_ref, sems)


def one_table(tables_in, half):
    words = TABLES[1] * TABLES[2]
    return tables_in.at[pl.ds(pl.multiple_of(half * words, words), words)]


def far_kernel(tables_in, halo_ref, _, out_ref, store, table_ref, squares_ref, sems):
    me = lax.axis_index("rows")
    core = lax.rem(me, 2)
    fetch = pltpu.make_async_copy(one_table(tables_in, 1 - core), table_ref, sems.at[0])

    @pl.when(me != 1)
    def _():
        fetch.start()

    fill(store, 3 * (1 - core), halo_ref)

    def put(i, block):
        out_ref[i] = block

    @pl.when(me != 1)
    def _():
        fetch.wait()
        rows = columns_of(table_ref.__getitem__, 2 - core)
        squares(table_ref.__getitem__, store, 2 - core, rows, rounded(squares_ref))
        cubes(table_ref.__getitem__, store, squares_ref, rows, put)


def near_kernel(
    tables_in, halo_ref, far_in, early_ref, _, out_ref, store, table_ref, far_table, squares_ref, sems, near, far
):
    me = lax.axis_index("rows")
    core = lax.rem(me, 2)
    fetch = pltpu.make_async_copy(one_table(tables_in, core), table_ref, sems.at[0])
    fetch.start()
    fetch_far = pltpu.make_async_copy(one_table(tables_in, 1 - core), far_table, sems.at[1])
    near_at = out_ref.at[pl.ds(core * HALF, HALF), 0]
    far_at = out_ref.at[pl.ds((1 - core) * HALF, HALF), 0]
    near_out = pltpu.make_async_copy(near, near_at, sems.at[2])
    far_out = pltpu.make_async_copy(far_in, far_at, sems.at[3])
    late_out = pltpu.make_async_copy(far, far_at, sems.at[3])

    @pl.when(me != 1)
    def _():
        far_out.start()

    @pl.when(me == 1)
    def _():
        fetch_far.start()

    fill(store, 3 * core, halo_ref)
    fetch.wait()
    rows = columns_of(table_ref.__getitem__, 1 + core)

    def put(i, block):
        near[i] = block
        pltpu.make_async_copy(near.at[i], near_at.at[i], sems.at[2]).start()

    @pl.when(me == 0)
    def _():
        low_halo_squares(table_ref.__getitem__, store, rows, rounded(squares_ref, early_ref))
        cubes(table_ref.__getitem__, store, squares_ref, rows, put)

    @pl.when(me != 0)
    def _():
        squares(table_ref.__getitem__, store, 1 + core, rows, rounded(squares_ref))
        cubes(table_ref.__getitem__, store, squares_ref, rows, put)

    @pl.when(me == 1)
    def _():
        def put_far(i, block):
            far[i] = block

        fetch_far.wait()
        far_rows = columns_of(far_table.__getitem__, 2 - core)
        squares(far_table.__getitem__, store, 2 - core, far_rows, rounded(squares_ref))
        cubes(far_table.__getitem__, store, squares_ref, far_rows, put_far)
        late_out.start()
        late_out.wait()

    @pl.when(me != 1)
    def _():
        far_out.wait()

    near_out.wait()


def vmem():
    return pl.BlockSpec(memory_space=pltpu.VMEM)


def hbm():
    return pl.BlockSpec(memory_space=pltpu.HBM)


def call(kernel, name, args, in_specs, out_shape, out_specs, scratch_shapes=(), aliases=None):
    return pl.pallas_call(
        kernel,
        out_shape=out_shape,
        in_specs=in_specs,
        out_specs=out_specs,
        scratch_shapes=scratch_shapes,
        input_output_aliases=aliases or {},
        compiler_params=pltpu.CompilerParams(vmem_limit_bytes=16 * 1024 * 1024),
        cost_estimate=pl.CostEstimate(flops=0, bytes_accessed=0, transcendentals=0),
        name=name,
    )(*args)


def local(block_values, pattern_cols, pattern_counts):
    count = lax.axis_size("rows")
    to_core = [(i, i ^ 1) for i in range(count)]
    to_chip = [(i, (i + 1 if i % 2 else i - 1) % count) for i in range(count)]
    bf16, i32 = jnp.bfloat16, jnp.int32
    block_values = pltpu.with_memory_space_constraint(block_values, pltpu.HBM)
    rows = [pltpu.VMEM((HALF, 8, 64, 64), bf16)]
    sems = [pltpu.SemaphoreType.DMA((HALF // PIECE,))]
    packed = [jax.ShapeDtypeStruct((HALF * 4 * TILE + pad, 128), bf16) for pad in (PAD, 0)]
    cols, counts = pattern_cols.T, pattern_counts.reshape(-1, 128)
    cols, counts = (pltpu.with_memory_space_constraint(x, pltpu.HBM) for x in (cols, counts))
    pattern = [pltpu.VMEM(cols.shape, i32), pltpu.VMEM(counts.shape, i32), pltpu.SemaphoreType.DMA((2,))]
    stored = [jax.ShapeDtypeStruct(TABLES, i32), jax.ShapeDtypeStruct(STORE, bf16)]
    near, far, tables, store, early = call(
        pack_kernel,
        "pack",
        [block_values, cols, counts],
        [hbm()] * 3,
        packed + stored + [jax.ShapeDtypeStruct((HALF, 64, 512), jnp.float32)],
        [vmem()] * 5,
        rows * 2 + sems * 2 + pattern + [pltpu.SMEM(TABLES[1:], i32), pltpu.SemaphoreType.DMA],
    )
    far = call(
        rest_kernel,
        "rest",
        [block_values, far],
        [hbm(), vmem()],
        packed[1],
        vmem(),
        rows + sems,
        {1: 0},
    )
    near_halo = lax.ppermute(near, "rows", to_chip)
    far_halo = lax.ppermute(far, "rows", to_core)
    tables, store = call(
        own_kernel,
        "own",
        [near, far, cols, counts, tables, store],
        [vmem(), vmem(), hbm(), hbm(), vmem(), vmem()],
        stored,
        [vmem()] * 2,
        pattern,
        {4: 0, 5: 1},
    )
    tables = tables.reshape(-1)
    scratch = [
        pltpu.SMEM((TABLES[1] * TABLES[2],), i32),
        pltpu.VMEM((HALF, 64, 512), bf16),
        pltpu.SemaphoreType.DMA((4,)),
    ]
    far_result, store = call(
        far_kernel,
        "far_half",
        [tables, far_halo, store],
        [vmem()] * 3,
        [jax.ShapeDtypeStruct((HALF, 64, 64), bf16), stored[1]],
        [vmem()] * 2,
        scratch,
        {2: 1},
    )
    result, _ = call(
        near_kernel,
        "near_half",
        [tables, near_halo, far_result, early, store],
        [vmem()] * 5,
        [jax.ShapeDtypeStruct((2 * HALF, 1, 64, 64), bf16), stored[1]],
        [hbm(), vmem()],
        [scratch[0], *scratch, *[pltpu.VMEM((HALF, 64, 64), bf16)] * 2],
        {4: 1},
    )
    return result


def solution(mesh):
    in_specs = (P("rows", None, None, None), P(), P())
    out_specs = P("rows", "rep", None, None)
    return jax.shard_map(local, mesh=mesh, in_specs=in_specs, out_specs=out_specs, check_vma=False)
```

```python
import functools

import jax
import jax.numpy as jnp
from jax import lax
from jax.experimental import pallas as pl
from jax.experimental.pallas import tpu as pltpu
from jax.sharding import PartitionSpec as P

HALF = 8
PIECE = 4
WINDOW = 32
TILE = 64
PAD = 16
GROUP = 12
ZERO_TILE = WINDOW * GROUP
STORE = (ZERO_TILE + 8, TILE, 128)
TABLES = (2, 8, 128)
DEAD = (WINDOW - 1, 0)
COLUMN_LINE = (6, 1)


def fill(store, chunk, ref):
    for row in range(HALF):
        base = (chunk * HALF + row) * GROUP
        for pair in range(4):
            tile = ref[pl.ds((row * 4 + pair) * TILE, TILE), :]
            store[base + pair] = tile
            store[base + 4 + pair] = pltpu.roll(tile, 64, 1)
            store[base + 8 + pair] = tile


def from_pieces(x_ref, rows, sems, starts):
    return [
        pltpu.make_async_copy(x_ref.at[pl.ds(start, PIECE)], rows.at[pl.ds(n * PIECE, PIECE)], sems.at[n])
        for n, start in enumerate(starts)
    ]


def pack(copies, rows, out_ref):
    for n, copy in enumerate(copies):
        copy.wait()
        for row in range(n * PIECE, (n + 1) * PIECE):
            for pair in range(4):
                at = pl.ds((row * 4 + pair) * TILE, TILE)
                blocks = [rows[row, 2 * pair + side] for side in range(2)]
                out_ref[at, :] = jnp.concatenate(blocks, axis=1)


def rest_kernel(x_ref, _, far_ref, far_rows, far_sems):
    me = lax.axis_index("rows")
    core = lax.rem(me, 2)

    @pl.when(me == lax.axis_size("rows") - 1)
    def _():
        far = from_pieces(x_ref, far_rows, far_sems, ((1 - core) * HALF, (1 - core) * HALF + PIECE))
        for copy in far:
            copy.start()
        pack(far, far_rows, far_ref)


def own(near_ref, far_ref, cols_in, counts_in, table_ref, store, cols_ref, counts_ref, sems):
    copies = [
        pltpu.make_async_copy(cols_in, cols_ref, sems.at[0]),
        pltpu.make_async_copy(counts_in, counts_ref, sems.at[1]),
    ]
    for copy in copies:
        copy.start()
    core = lax.rem(lax.axis_index("rows"), 2)
    zeros = jnp.zeros((TILE, 128), jnp.bfloat16)
    store[ZERO_TILE] = zeros
    store[ZERO_TILE + 4] = zeros
    fill(store, 1 + core, near_ref)
    fill(store, 2 - core, far_ref)
    for copy in copies:
        copy.wait()
    total = cols_ref.shape[1]
    chunks = total // 128
    start = lax.rem(lax.axis_index("rows") * (2 * HALF) + (total - HALF), total)
    first = lax.div(start, 128)
    second = lax.rem(first + 1, chunks)
    shift = lax.rem(256 - lax.rem(start, 128), 256)

    def window(get):
        both = jnp.concatenate([get(first), get(second)], axis=1)
        return pltpu.roll(both, shift, 1)[:, :128]

    cols = window(lambda k: cols_ref[:, pl.ds(pl.multiple_of(k * 128, 128), 128)])
    counts = window(lambda k: jnp.broadcast_to(counts_ref[pl.ds(k, 1), :], (8, 128)))
    relative = cols - start
    relative = jnp.where(relative < 0, relative + total, relative)
    slot = lax.broadcasted_iota(jnp.int32, (8, 128), 0)
    lane = lax.broadcasted_iota(jnp.int32, (8, 128), 1)
    live = (slot < counts) & (lane < WINDOW)
    matchable = jnp.where(live & (relative < WINDOW), relative, -1)
    matchable = functools.reduce(
        jnp.maximum, [matchable] + [pltpu.roll(matchable, by, 1) for by in (32, 64, 96)]
    )
    column = slot * 4 + lane // WINDOW
    row = lane % WINDOW
    tiles = jnp.full((8, 128), ZERO_TILE, jnp.int32)
    for s in range(8):
        here = jnp.broadcast_to(matchable[s : s + 1, :], (8, 128)) == column
        tiles = jnp.where(here, row * GROUP + ((s % 2) * 4 + s // 2), tiles)
    reached = ((column < 24) & (row < 24), (column >= 8) & (row >= 8))
    for high in range(2):
        columns = jnp.where(live, relative, DEAD[high])
        line = jnp.zeros((8, 128), jnp.int32)
        for s in range(8):
            moved = pltpu.roll(columns, (s * 8 - HALF * (1 + high)) % 128, 1)
            line = jnp.where(lane // 8 == s, jnp.broadcast_to(moved[s : s + 1, :], (8, 128)), line)
        words = jnp.where(reached[high], tiles, ZERO_TILE)
        table_ref[high] = jnp.where(slot == COLUMN_LINE[high], line, words)


def columns_of(word, center):
    mine = lax.axis_index("rep")
    start = jnp.where(center == 1, COLUMN_LINE[0], COLUMN_LINE[1]) * 128
    return [
        [word(start + (mine ^ q) * 8 + i) for q in range(8)] for i in range(HALF)
    ]


def left_side():
    return lax.broadcasted_iota(jnp.int16, (TILE, 128), 1) < 64


def gathered(word, store, left, cols, sources, n):
    def tile(p, source):
        one = word(cols[2 * p] * WINDOW + source)
        two = word(cols[2 * p + 1] * WINDOW + source)
        return jnp.where(left, store[one], store[two + 4])

    return jnp.concatenate(
        [jnp.concatenate([tile(2 * n + j, b) for j in range(2)], axis=1) for b in sources], axis=0
    )


def product(x, word, store, left, cols, sources, n):
    total = None
    for k in range(0, len(sources), 4):
        g = gathered(word, store, left, cols, sources[k : k + 4], n)
        part = jnp.dot(x[:, k * 64 : (k + 4) * 64], g, preferred_element_type=jnp.float32)
        total = part if total is None else total + part
    return total


def squares(word, store, center, rows, put, skip=None):
    mine = lax.axis_index("rep")
    left = left_side()
    for i in range(HALF):
        at = (center * HALF + i) * GROUP + lax.rem(mine, 2) * 4
        x = jnp.concatenate([store[at + (lax.div(mine, 2) ^ p)] for p in range(4)], axis=1)
        sources = rows[i]
        if skip is not None:
            sources = [jnp.where(lax.div(c, HALF) == skip, DEAD[0], c) for c in sources]
        for n in range(2):
            put(i, n, product(x, word, store, left, rows[i], sources, n))


def low_halo_squares(word, store, rows, put):
    left = left_side()
    for i in range(HALF):
        sources = list(range(i, HALF + i % 2))
        found = [word(w * WINDOW + HALF + i) if w < HALF else ZERO_TILE for w in sources]
        x = jnp.concatenate(
            [
                jnp.where(left, store[found[k]], store[found[k + 1] + 4])
                for k in range(0, len(sources), 2)
            ],
            axis=1,
        )
        for n in range(2):
            put(i, n, product(x, word, store, left, rows[i], sources, n))


def cubes(word, store, squares_ref, rows, put):
    for i in range(HALF):
        cube = None
        for k in range(2):
            g = jnp.concatenate(
                [store[word(rows[i][0] * WINDOW + c)] for c in rows[i][4 * k : 4 * k + 4]], axis=0
            )
            part = jnp.dot(
                squares_ref[i, :, k * 256 : (k + 1) * 256], g, preferred_element_type=jnp.float32
            )
            cube = part if cube is None else cube + part
        purified = 3.0 * squares_ref[i, :, 0:128].astype(jnp.float32) - 2.0 * cube
        put(i, purified[:, :64].astype(jnp.bfloat16))


def rounded(squares_ref, before=None):
    def put(i, n, total):
        at = slice(n * 256, (n + 1) * 256)
        if before is not None:
            total = total + before[i, :, at]
        squares_ref[i, :, at] = total.astype(jnp.bfloat16)

    return put


def waits_longest():
    return (lax.axis_index("rows") == 0) & (lax.axis_index("rep") != 0)


def pack_kernel(
    x_ref,
    cols_in,
    counts_in,
    near_ref,
    far_ref,
    tables_ref,
    store,
    early_ref,
    near_rows,
    far_rows,
    near_sems,
    far_sems,
    cols_ref,
    counts_ref,
    own_sems,
    table_ref,
    fetch_sem,
):
    me = lax.axis_index("rows")
    core = lax.rem(me, 2)
    late = me == lax.axis_size("rows") - 1
    near = from_pieces(x_ref, near_rows, near_sems, (core * HALF, core * HALF + PIECE))
    far = from_pieces(x_ref, far_rows, far_sems, ((1 - core) * HALF, (1 - core) * HALF + PIECE))
    for copy in near:
        copy.start()

    @pl.when(jnp.logical_not(late))
    def _():
        for copy in far:
            copy.start()

    near_ref[HALF * 4 * TILE :, :] = jnp.zeros((PAD, 128), jnp.bfloat16)
    pack(near, near_rows, near_ref)

    @pl.when(jnp.logical_not(late))
    def _():
        pack(far, far_rows, far_ref)

    @pl.when(waits_longest())
    def _():
        own(near_ref, far_ref, cols_in, counts_in, tables_ref, store, cols_ref, counts_ref, own_sems)
        fetch = pltpu.make_async_copy(tables_ref.at[0], table_ref, fetch_sem)
        fetch.start()
        fetch.wait()

        def word(at):
            return table_ref[lax.div(at, 128), lax.rem(at, 128)]

        def put(i, n, total):
            early_ref[i, :, n * 256 : (n + 1) * 256] = total

        squares(word, store, 1, columns_of(word, 1), put, skip=0)


def own_kernel(near_ref, far_ref, cols_in, counts_in, _, __, tables_ref, store, cols_ref, counts_ref, sems):
    @pl.when(jnp.logical_not(waits_longest()))
    def _():
        own(near_ref, far_ref, cols_in, counts_in, tables_ref, store, cols_ref, counts_ref, sems)


def one_table(tables_in, half):
    words = TABLES[1] * TABLES[2]
    return tables_in.at[pl.ds(pl.multiple_of(half * words, words), words)]


def far_kernel(tables_in, halo_ref, _, out_ref, store, table_ref, squares_ref, sems):
    me = lax.axis_index("rows")
    core = lax.rem(me, 2)
    fetch = pltpu.make_async_copy(one_table(tables_in, 1 - core), table_ref, sems.at[0])

    @pl.when(me != 1)
    def _():
        fetch.start()

    fill(store, 3 * (1 - core), halo_ref)

    def put(i, block):
        out_ref[i] = block

    @pl.when(me != 1)
    def _():
        fetch.wait()
        rows = columns_of(table_ref.__getitem__, 2 - core)
        squares(table_ref.__getitem__, store, 2 - core, rows, rounded(squares_ref))
        cubes(table_ref.__getitem__, store, squares_ref, rows, put)


def near_kernel(
    tables_in, halo_ref, far_in, early_ref, _, out_ref, store, table_ref, far_table, squares_ref, sems, near, far
):
    me = lax.axis_index("rows")
    core = lax.rem(me, 2)
    fetch = pltpu.make_async_copy(one_table(tables_in, core), table_ref, sems.at[0])
    fetch.start()
    fetch_far = pltpu.make_async_copy(one_table(tables_in, 1 - core), far_table, sems.at[1])
    near_at = out_ref.at[pl.ds(core * HALF, HALF), 0]
    far_at = out_ref.at[pl.ds((1 - core) * HALF, HALF), 0]
    near_out = pltpu.make_async_copy(near, near_at, sems.at[2])
    far_out = pltpu.make_async_copy(far_in, far_at, sems.at[3])
    late_out = pltpu.make_async_copy(far, far_at, sems.at[3])

    @pl.when(me != 1)
    def _():
        far_out.start()

    @pl.when(me == 1)
    def _():
        fetch_far.start()

    fill(store, 3 * core, halo_ref)
    fetch.wait()
    rows = columns_of(table_ref.__getitem__, 1 + core)

    def put(i, block):
        near[i] = block
        pltpu.make_async_copy(near.at[i], near_at.at[i], sems.at[2]).start()

    @pl.when(waits_longest())
    def _():
        low_halo_squares(table_ref.__getitem__, store, rows, rounded(squares_ref, early_ref))
        cubes(table_ref.__getitem__, store, squares_ref, rows, put)

    @pl.when(jnp.logical_not(waits_longest()))
    def _():
        squares(table_ref.__getitem__, store, 1 + core, rows, rounded(squares_ref))
        cubes(table_ref.__getitem__, store, squares_ref, rows, put)

    @pl.when(me == 1)
    def _():
        def put_far(i, block):
            far[i] = block

        fetch_far.wait()
        far_rows = columns_of(far_table.__getitem__, 2 - core)
        squares(far_table.__getitem__, store, 2 - core, far_rows, rounded(squares_ref))
        cubes(far_table.__getitem__, store, squares_ref, far_rows, put_far)
        late_out.start()
        late_out.wait()

    @pl.when(me != 1)
    def _():
        far_out.wait()

    near_out.wait()


def vmem():
    return pl.BlockSpec(memory_space=pltpu.VMEM)


def hbm():
    return pl.BlockSpec(memory_space=pltpu.HBM)


def call(kernel, name, args, in_specs, out_shape, out_specs, scratch_shapes=(), aliases=None):
    return pl.pallas_call(
        kernel,
        out_shape=out_shape,
        in_specs=in_specs,
        out_specs=out_specs,
        scratch_shapes=scratch_shapes,
        input_output_aliases=aliases or {},
        compiler_params=pltpu.CompilerParams(vmem_limit_bytes=16 * 1024 * 1024),
        cost_estimate=pl.CostEstimate(flops=0, bytes_accessed=0, transcendentals=0),
        name=name,
    )(*args)


def local(block_values, pattern_cols, pattern_counts):
    count = lax.axis_size("rows")
    to_core = [(i, i ^ 1) for i in range(count)]
    to_chip = [(i, (i + 1 if i % 2 else i - 1) % count) for i in range(count)]
    bf16, i32 = jnp.bfloat16, jnp.int32
    block_values = pltpu.with_memory_space_constraint(block_values, pltpu.HBM)
    rows = [pltpu.VMEM((HALF, 8, 64, 64), bf16)]
    sems = [pltpu.SemaphoreType.DMA((HALF // PIECE,))]
    packed = [jax.ShapeDtypeStruct((HALF * 4 * TILE + pad, 128), bf16) for pad in (PAD, 0)]
    cols, counts = pattern_cols.T, pattern_counts.reshape(-1, 128)
    cols, counts = (pltpu.with_memory_space_constraint(x, pltpu.HBM) for x in (cols, counts))
    pattern = [pltpu.VMEM(cols.shape, i32), pltpu.VMEM(counts.shape, i32), pltpu.SemaphoreType.DMA((2,))]
    stored = [jax.ShapeDtypeStruct(TABLES, i32), jax.ShapeDtypeStruct(STORE, bf16)]
    near, far, tables, store, early = call(
        pack_kernel,
        "pack",
        [block_values, cols, counts],
        [hbm()] * 3,
        packed + stored + [jax.ShapeDtypeStruct((HALF, 64, 512), jnp.float32)],
        [vmem()] * 5,
        rows * 2 + sems * 2 + pattern + [pltpu.SMEM(TABLES[1:], i32), pltpu.SemaphoreType.DMA],
    )
    far = call(
        rest_kernel,
        "rest",
        [block_values, far],
        [hbm(), vmem()],
        packed[1],
        vmem(),
        rows + sems,
        {1: 0},
    )
    near_halo = lax.ppermute(near, "rows", to_chip)
    far_halo = lax.ppermute(far, "rows", to_core)
    tables, store = call(
        own_kernel,
        "own",
        [near, far, cols, counts, tables, store],
        [vmem(), vmem(), hbm(), hbm(), vmem(), vmem()],
        stored,
        [vmem()] * 2,
        pattern,
        {4: 0, 5: 1},
    )
    tables = tables.reshape(-1)
    scratch = [
        pltpu.SMEM((TABLES[1] * TABLES[2],), i32),
        pltpu.VMEM((HALF, 64, 512), bf16),
        pltpu.SemaphoreType.DMA((4,)),
    ]
    far_result, store = call(
        far_kernel,
        "far_half",
        [tables, far_halo, store],
        [vmem()] * 3,
        [jax.ShapeDtypeStruct((HALF, 64, 64), bf16), stored[1]],
        [vmem()] * 2,
        scratch,
        {2: 1},
    )
    result, _ = call(
        near_kernel,
        "near_half",
        [tables, near_halo, far_result, early, store],
        [vmem()] * 5,
        [jax.ShapeDtypeStruct((2 * HALF, 1, 64, 64), bf16), stored[1]],
        [hbm(), vmem()],
        [scratch[0], *scratch, *[pltpu.VMEM((HALF, 64, 64), bf16)] * 2],
        {4: 1},
    )
    return result


def solution(mesh):
    in_specs = (P("rows", None, None, None), P(), P())
    out_specs = P("rows", "rep", None, None)
    return jax.shard_map(local, mesh=mesh, in_specs=in_specs, out_specs=out_specs, check_vma=False)
```

```python
import jax
import jax.numpy as jnp
from jax import lax
from jax.experimental import pallas as pl
from jax.experimental.pallas import tpu as pltpu
from jax.sharding import PartitionSpec as P

HALF = 8
PIECE = 4
WINDOW = 32
TILE = 64
PAD = 16
GROUP = 12
ZERO_TILE = WINDOW * GROUP
STORE = (ZERO_TILE + 8, TILE, 128)
ALL, EARLY, LOW, LOW_X = range(4)
LISTS = (4, 8, 128)


def fill(store, chunk, ref):
    for row in range(HALF):
        base = (chunk * HALF + row) * GROUP
        for pair in range(4):
            tile = ref[pl.ds((row * 4 + pair) * TILE, TILE), :]
            store[base + pair] = tile
            store[base + 4 + pair] = pltpu.roll(tile, 64, 1)
            store[base + 8 + pair] = tile


def from_pieces(x_ref, rows, sems, starts):
    return [
        pltpu.make_async_copy(x_ref.at[pl.ds(start, PIECE)], rows.at[pl.ds(n * PIECE, PIECE)], sems.at[n])
        for n, start in enumerate(starts)
    ]


def pack(copies, rows, out_ref):
    for n, copy in enumerate(copies):
        copy.wait()
        for row in range(n * PIECE, (n + 1) * PIECE):
            for pair in range(4):
                at = pl.ds((row * 4 + pair) * TILE, TILE)
                blocks = [rows[row, 2 * pair + side] for side in range(2)]
                out_ref[at, :] = jnp.concatenate(blocks, axis=1)


def rest_kernel(x_ref, _, far_ref, far_rows, far_sems):
    me = lax.axis_index("rows")
    core = lax.rem(me, 2)

    @pl.when(me == lax.axis_size("rows") - 1)
    def _():
        far = from_pieces(x_ref, far_rows, far_sems, ((1 - core) * HALF, (1 - core) * HALF + PIECE))
        for copy in far:
            copy.start()
        pack(far, far_rows, far_ref)


def own(near_ref, far_ref, cols_in, counts_in, lists_ref, store, cols_ref, counts_ref, sems):
    copies = [
        pltpu.make_async_copy(cols_in, cols_ref, sems.at[0]),
        pltpu.make_async_copy(counts_in, counts_ref, sems.at[1]),
    ]
    for copy in copies:
        copy.start()
    core = lax.rem(lax.axis_index("rows"), 2)
    zeros = jnp.zeros((TILE, 128), jnp.bfloat16)
    store[ZERO_TILE] = zeros
    store[ZERO_TILE + 4] = zeros
    fill(store, 1 + core, near_ref)
    fill(store, 2 - core, far_ref)
    for copy in copies:
        copy.wait()
    total = cols_ref.shape[1]
    chunks = total // 128
    start = lax.rem(lax.axis_index("rows") * (2 * HALF) + (total - HALF), total)
    first = lax.div(start, 128)
    second = lax.rem(first + 1, chunks)
    shift = lax.rem(256 - lax.rem(start, 128), 256)

    def window(get):
        both = jnp.concatenate([get(first), get(second)], axis=1)
        return pltpu.roll(both, shift, 1)[:, :128]

    cols = window(lambda k: cols_ref[:, pl.ds(pl.multiple_of(k * 128, 128), 128)])
    counts = window(lambda k: jnp.broadcast_to(counts_ref[pl.ds(k, 1), :], (8, 128)))
    relative = cols - start
    relative = jnp.where(relative < 0, relative + total, relative)
    slot = lax.broadcasted_iota(jnp.int32, (8, 128), 0)
    lane = lax.broadcasted_iota(jnp.int32, (8, 128), 1)
    live = (slot < counts) & (lane < WINDOW) & (relative < WINDOW)
    columns = jnp.where(live, relative, -1)
    side = (slot % 2) * 4 + slot // 2
    mine = lax.axis_index("rep")

    def at_lanes(which):
        return jnp.take_along_axis(columns, which, axis=1, mode="promise_in_bounds")

    def highest(x):
        return jnp.broadcast_to(jnp.max(x, axis=0, keepdims=True), (8, 128))

    def tiles(own, row):
        found = at_lanes(jnp.maximum(row, 0))
        result = jnp.full((8, 128), ZERO_TILE, jnp.int32)
        for q in range(8):
            wanted = highest(jnp.where(slot == (mine ^ q), own, -1))
            match = (found == wanted) & (wanted >= 0) & (row >= 0)
            tile = highest(jnp.where(match, row * GROUP + side, -1))
            result = jnp.where((slot == q) & (tile >= 0), tile, result)
        return result

    own_row = HALF + lane // 8
    own_columns = at_lanes(own_row)
    source = highest(jnp.where(slot == ((lane % 8) ^ mine), own_columns, -1))
    everything = tiles(own_columns, source)
    lists_ref[ALL] = everything
    lists_ref[EARLY] = jnp.where(source < HALF, ZERO_TILE, everything)
    lists_ref[LOW] = tiles(own_columns, lane % 8)
    low_x = highest(jnp.where(own_columns == lane % 8, own_row * GROUP + side, -1))
    lists_ref[LOW_X] = jnp.where(low_x >= 0, low_x, ZERO_TILE)


def half_list(lists_ref, center):
    return jnp.where(center == 1, lists_ref[ALL], pltpu.roll(lists_ref[ALL], 64, 1))


def product(x, tiles, store, sources, n):
    left = lax.broadcasted_iota(jnp.int16, (TILE, 128), 1) < 64

    def tile(p, b):
        if b is None:
            return jnp.zeros((TILE, 128), jnp.bfloat16)
        return jnp.where(left, store[tiles[2 * p, b]], store[tiles[2 * p + 1, b] + 4])

    total = None
    for k in range(0, len(sources), 4):
        g = jnp.concatenate(
            [
                jnp.concatenate([tile(2 * n + j, b) for j in range(2)], axis=1)
                for b in sources[k : k + 4]
            ],
            axis=0,
        )
        part = jnp.dot(x[:, k * 64 : (k + 4) * 64], g, preferred_element_type=jnp.float32)
        total = part if total is None else total + part
    return total


def squares(tiles, store, center, put):
    mine = lax.axis_index("rep")
    for i in range(HALF):
        at = (center * HALF + i) * GROUP + lax.rem(mine, 2) * 4
        x = jnp.concatenate([store[at + (lax.div(mine, 2) ^ p)] for p in range(4)], axis=1)
        for n in range(2):
            put(i, n, product(x, tiles, store, [i * 8 + b for b in range(8)], n))


def low_halo_squares(lists_ref, store, put):
    tiles, own_tiles = lists_ref[LOW], lists_ref[LOW_X]
    left = lax.broadcasted_iota(jnp.int16, (TILE, 128), 1) < 64
    for i in range(HALF):
        sources = [i * 8 + w for w in range(i, HALF)] + [None] * (i % 2)
        found = [ZERO_TILE if b is None else own_tiles[0, b] for b in sources]
        x = jnp.concatenate(
            [
                jnp.where(left, store[found[k]], store[found[k + 1] + 4])
                for k in range(0, len(sources), 2)
            ],
            axis=1,
        )
        for n in range(2):
            put(i, n, product(x, tiles, store, sources, n))


def cubes(tiles, store, squares_ref, put):
    for i in range(HALF):
        cube = None
        for k in range(2):
            g = jnp.concatenate([store[tiles[0, i * 8 + 4 * k + b]] for b in range(4)], axis=0)
            part = jnp.dot(
                squares_ref[i, :, k * 256 : (k + 1) * 256], g, preferred_element_type=jnp.float32
            )
            cube = part if cube is None else cube + part
        purified = 3.0 * squares_ref[i, :, 0:128].astype(jnp.float32) - 2.0 * cube
        put(i, purified[:, :64].astype(jnp.bfloat16))


def rounded(squares_ref, before=None):
    def put(i, n, total):
        at = slice(n * 256, (n + 1) * 256)
        if before is not None:
            total = total + before[i, :, at]
        squares_ref[i, :, at] = total.astype(jnp.bfloat16)

    return put


def waits_longest():
    return (lax.axis_index("rows") == 0) & (lax.axis_index("rep") != 0)


def pack_kernel(
    x_ref,
    cols_in,
    counts_in,
    near_ref,
    far_ref,
    lists_ref,
    store,
    early_ref,
    near_rows,
    far_rows,
    near_sems,
    far_sems,
    cols_ref,
    counts_ref,
    own_sems,
):
    me = lax.axis_index("rows")
    core = lax.rem(me, 2)
    late = me == lax.axis_size("rows") - 1
    near = from_pieces(x_ref, near_rows, near_sems, (core * HALF, core * HALF + PIECE))
    far = from_pieces(x_ref, far_rows, far_sems, ((1 - core) * HALF, (1 - core) * HALF + PIECE))
    for copy in near:
        copy.start()

    @pl.when(jnp.logical_not(late))
    def _():
        for copy in far:
            copy.start()

    near_ref[HALF * 4 * TILE :, :] = jnp.zeros((PAD, 128), jnp.bfloat16)
    pack(near, near_rows, near_ref)

    @pl.when(jnp.logical_not(late))
    def _():
        pack(far, far_rows, far_ref)

    @pl.when(waits_longest())
    def _():
        own(near_ref, far_ref, cols_in, counts_in, lists_ref, store, cols_ref, counts_ref, own_sems)

        def put(i, n, total):
            early_ref[i, :, n * 256 : (n + 1) * 256] = total

        squares(lists_ref[EARLY], store, 1, put)


def own_kernel(near_ref, far_ref, cols_in, counts_in, _, __, lists_ref, store, cols_ref, counts_ref, sems):
    @pl.when(jnp.logical_not(waits_longest()))
    def _():
        own(near_ref, far_ref, cols_in, counts_in, lists_ref, store, cols_ref, counts_ref, sems)


def far_kernel(lists_ref, halo_ref, _, out_ref, store, squares_ref):
    me = lax.axis_index("rows")
    core = lax.rem(me, 2)
    fill(store, 3 * (1 - core), halo_ref)

    def put(i, block):
        out_ref[i] = block

    @pl.when(me != 1)
    def _():
        tiles = half_list(lists_ref, 2 - core)
        squares(tiles, store, 2 - core, rounded(squares_ref))
        cubes(tiles, store, squares_ref, put)


def near_kernel(lists_ref, halo_ref, far_in, early_ref, _, out_ref, store, squares_ref, near, far, sems):
    me = lax.axis_index("rows")
    core = lax.rem(me, 2)
    near_at = out_ref.at[pl.ds(core * HALF, HALF), 0]
    far_at = out_ref.at[pl.ds((1 - core) * HALF, HALF), 0]
    near_out = pltpu.make_async_copy(near, near_at, sems.at[0])
    far_out = pltpu.make_async_copy(far_in, far_at, sems.at[1])
    late_out = pltpu.make_async_copy(far, far_at, sems.at[1])

    @pl.when(me != 1)
    def _():
        far_out.start()

    fill(store, 3 * core, halo_ref)

    def put(i, block):
        near[i] = block

    @pl.when(waits_longest())
    def _():
        low_halo_squares(lists_ref, store, rounded(squares_ref, early_ref))
        cubes(lists_ref[ALL], store, squares_ref, put)

    @pl.when(jnp.logical_not(waits_longest()))
    def _():
        tiles = half_list(lists_ref, 1 + core)
        squares(tiles, store, 1 + core, rounded(squares_ref))
        cubes(tiles, store, squares_ref, put)

    near_out.start()

    @pl.when(me == 1)
    def _():
        def put_far(i, block):
            far[i] = block

        tiles = half_list(lists_ref, 2 - core)
        squares(tiles, store, 2 - core, rounded(squares_ref))
        cubes(tiles, store, squares_ref, put_far)
        late_out.start()
        late_out.wait()

    @pl.when(me != 1)
    def _():
        far_out.wait()

    near_out.wait()


def vmem():
    return pl.BlockSpec(memory_space=pltpu.VMEM)


def hbm():
    return pl.BlockSpec(memory_space=pltpu.HBM)


def call(kernel, name, args, in_specs, out_shape, out_specs, scratch_shapes=(), aliases=None):
    return pl.pallas_call(
        kernel,
        out_shape=out_shape,
        in_specs=in_specs,
        out_specs=out_specs,
        scratch_shapes=scratch_shapes,
        input_output_aliases=aliases or {},
        compiler_params=pltpu.CompilerParams(vmem_limit_bytes=16 * 1024 * 1024),
        cost_estimate=pl.CostEstimate(flops=0, bytes_accessed=0, transcendentals=0),
        name=name,
    )(*args)


def local(block_values, pattern_cols, pattern_counts):
    count = lax.axis_size("rows")
    to_core = [(i, i ^ 1) for i in range(count)]
    to_chip = [(i, (i + 1 if i % 2 else i - 1) % count) for i in range(count)]
    bf16, i32 = jnp.bfloat16, jnp.int32
    block_values = pltpu.with_memory_space_constraint(block_values, pltpu.HBM)
    rows = [pltpu.VMEM((HALF, 8, 64, 64), bf16)]
    sems = [pltpu.SemaphoreType.DMA((HALF // PIECE,))]
    packed = [jax.ShapeDtypeStruct((HALF * 4 * TILE + pad, 128), bf16) for pad in (PAD, 0)]
    cols, counts = pattern_cols.T, pattern_counts.reshape(-1, 128)
    cols, counts = (pltpu.with_memory_space_constraint(x, pltpu.HBM) for x in (cols, counts))
    pattern = [pltpu.VMEM(cols.shape, i32), pltpu.VMEM(counts.shape, i32), pltpu.SemaphoreType.DMA((2,))]
    stored = [jax.ShapeDtypeStruct(LISTS, i32), jax.ShapeDtypeStruct(STORE, bf16)]
    near, far, lists, store, early = call(
        pack_kernel,
        "pack",
        [block_values, cols, counts],
        [hbm()] * 3,
        packed + stored + [jax.ShapeDtypeStruct((HALF, 64, 512), jnp.float32)],
        [vmem()] * 5,
        rows * 2 + sems * 2 + pattern,
    )
    far = call(
        rest_kernel,
        "rest",
        [block_values, far],
        [hbm(), vmem()],
        packed[1],
        vmem(),
        rows + sems,
        {1: 0},
    )
    near_halo = lax.ppermute(near, "rows", to_chip)
    far_halo = lax.ppermute(far, "rows", to_core)
    lists, store = call(
        own_kernel,
        "own",
        [near, far, cols, counts, lists, store],
        [vmem(), vmem(), hbm(), hbm(), vmem(), vmem()],
        stored,
        [vmem()] * 2,
        pattern,
        {4: 0, 5: 1},
    )
    scratch = [pltpu.VMEM((HALF, 64, 512), bf16)]
    far_result, store = call(
        far_kernel,
        "far_half",
        [lists, far_halo, store],
        [vmem()] * 3,
        [jax.ShapeDtypeStruct((HALF, 64, 64), bf16), stored[1]],
        [vmem()] * 2,
        scratch,
        {2: 1},
    )
    result, _ = call(
        near_kernel,
        "near_half",
        [lists, near_halo, far_result, early, store],
        [vmem()] * 5,
        [jax.ShapeDtypeStruct((2 * HALF, 1, 64, 64), bf16), stored[1]],
        [hbm(), vmem()],
        scratch + [pltpu.VMEM((HALF, 64, 64), bf16)] * 2 + [pltpu.SemaphoreType.DMA((2,))],
        {4: 1},
    )
    return result


def solution(mesh):
    in_specs = (P("rows", None, None, None), P(), P())
    out_specs = P("rows", "rep", None, None)
    return jax.shard_map(local, mesh=mesh, in_specs=in_specs, out_specs=out_specs, check_vma=False)
```

```python
import jax
import jax.numpy as jnp
from jax import lax
from jax.experimental import pallas as pl
from jax.experimental.pallas import tpu as pltpu
from jax.sharding import PartitionSpec as P

HALF = 8
PIECE = 4
WINDOW = 32
TILE = 64
PAD = 16
GROUP = 8
ZERO_TILE = WINDOW * GROUP
STORE = (ZERO_TILE + 1, TILE, 128)
ALL, EARLY, LOW, LOW_X = range(4)
LISTS = (4, 8, 128)


def fill(store, chunk, ref):
    for row in range(HALF):
        base = (chunk * HALF + row) * GROUP
        for pair in range(4):
            tile = ref[pl.ds((row * 4 + pair) * TILE, TILE), :]
            store[base + pair] = tile
            store[base + 4 + pair] = pltpu.roll(tile, 64, 1)


def from_pieces(x_ref, rows, sems, starts):
    return [
        pltpu.make_async_copy(x_ref.at[pl.ds(start, PIECE)], rows.at[pl.ds(n * PIECE, PIECE)], sems.at[n])
        for n, start in enumerate(starts)
    ]


def pack(copies, rows, out_ref):
    for n, copy in enumerate(copies):
        copy.wait()
        for row in range(n * PIECE, (n + 1) * PIECE):
            for pair in range(4):
                at = pl.ds((row * 4 + pair) * TILE, TILE)
                blocks = [rows[row, 2 * pair + side] for side in range(2)]
                out_ref[at, :] = jnp.concatenate(blocks, axis=1)


def rest_kernel(x_ref, _, far_ref, far_rows, far_sems):
    me = lax.axis_index("rows")
    core = lax.rem(me, 2)

    @pl.when(me == lax.axis_size("rows") - 1)
    def _():
        far = from_pieces(x_ref, far_rows, far_sems, ((1 - core) * HALF, (1 - core) * HALF + PIECE))
        for copy in far:
            copy.start()
        pack(far, far_rows, far_ref)


def own(near_ref, far_ref, cols_in, counts_in, lists_ref, store, cols_ref, counts_ref, sems):
    copies = [
        pltpu.make_async_copy(cols_in, cols_ref, sems.at[0]),
        pltpu.make_async_copy(counts_in, counts_ref, sems.at[1]),
    ]
    for copy in copies:
        copy.start()
    core = lax.rem(lax.axis_index("rows"), 2)
    zeros = jnp.zeros((TILE, 128), jnp.bfloat16)
    store[ZERO_TILE] = zeros
    fill(store, 1 + core, near_ref)
    fill(store, 2 - core, far_ref)
    for copy in copies:
        copy.wait()
    total = cols_ref.shape[1]
    chunks = total // 128
    start = lax.rem(lax.axis_index("rows") * (2 * HALF) + (total - HALF), total)
    first = lax.div(start, 128)
    second = lax.rem(first + 1, chunks)
    shift = lax.rem(256 - lax.rem(start, 128), 256)

    def window(get):
        both = jnp.concatenate([get(first), get(second)], axis=1)
        return pltpu.roll(both, shift, 1)[:, :128]

    cols = window(lambda k: cols_ref[:, pl.ds(pl.multiple_of(k * 128, 128), 128)])
    counts = window(lambda k: jnp.broadcast_to(counts_ref[pl.ds(k, 1), :], (8, 128)))
    relative = cols - start
    relative = jnp.where(relative < 0, relative + total, relative)
    slot = lax.broadcasted_iota(jnp.int32, (8, 128), 0)
    lane = lax.broadcasted_iota(jnp.int32, (8, 128), 1)
    live = (slot < counts) & (lane < WINDOW) & (relative < WINDOW)
    columns = jnp.where(live, relative, -1)
    side = (slot % 2) * 4 + slot // 2
    mine = lax.axis_index("rep")

    def at_lanes(which):
        return jnp.take_along_axis(columns, which, axis=1, mode="promise_in_bounds")

    def highest(x):
        return jnp.broadcast_to(jnp.max(x, axis=0, keepdims=True), (8, 128))

    def tiles(own, row):
        found = at_lanes(jnp.maximum(row, 0))
        result = jnp.full((8, 128), ZERO_TILE, jnp.int32)
        for q in range(8):
            wanted = highest(jnp.where(slot == (mine ^ q), own, -1))
            match = (found == wanted) & (wanted >= 0) & (row >= 0)
            tile = highest(jnp.where(match, row * GROUP + (side ^ (q % 2 * 4)), -1))
            result = jnp.where((slot == q) & (tile >= 0), tile, result)
        return result

    own_row = HALF + lane // 8
    own_columns = at_lanes(own_row)
    source = highest(jnp.where(slot == ((lane % 8) ^ mine), own_columns, -1))
    everything = tiles(own_columns, source)
    lists_ref[ALL] = everything
    lists_ref[EARLY] = jnp.where(source < HALF, ZERO_TILE, everything)
    lists_ref[LOW] = tiles(own_columns, lane % 8)
    right = (lane % 8 + lane // 8) % 2 * 4
    low_x = highest(jnp.where(own_columns == lane % 8, own_row * GROUP + (side ^ right), -1))
    lists_ref[LOW_X] = jnp.where(low_x >= 0, low_x, ZERO_TILE)


def half_list(lists_ref, center):
    return jnp.where(center == 1, lists_ref[ALL], pltpu.roll(lists_ref[ALL], 64, 1))


def product(x, tiles, store, sources, n):
    left = lax.broadcasted_iota(jnp.int16, (TILE, 128), 1) < 64

    def tile(p, b):
        if b is None:
            return jnp.zeros((TILE, 128), jnp.bfloat16)
        return jnp.where(left, store[tiles[2 * p, b]], store[tiles[2 * p + 1, b]])

    total = None
    for k in range(0, len(sources), 4):
        g = jnp.concatenate(
            [
                jnp.concatenate([tile(2 * n + j, b) for j in range(2)], axis=1)
                for b in sources[k : k + 4]
            ],
            axis=0,
        )
        part = jnp.dot(x[:, k * 64 : (k + 4) * 64], g, preferred_element_type=jnp.float32)
        total = part if total is None else total + part
    return total


def squares(tiles, store, center, put):
    mine = lax.axis_index("rep")
    for i in range(HALF):
        at = (center * HALF + i) * GROUP + lax.rem(mine, 2) * 4
        x = jnp.concatenate([store[at + (lax.div(mine, 2) ^ p)] for p in range(4)], axis=1)
        for n in range(2):
            put(i, n, product(x, tiles, store, [i * 8 + b for b in range(8)], n))


def low_halo_squares(lists_ref, store, put):
    tiles, own_tiles = lists_ref[LOW], lists_ref[LOW_X]
    left = lax.broadcasted_iota(jnp.int16, (TILE, 128), 1) < 64
    for i in range(HALF):
        sources = [i * 8 + w for w in range(i, HALF)] + [None] * (i % 2)
        found = [ZERO_TILE if b is None else own_tiles[0, b] for b in sources]
        x = jnp.concatenate(
            [
                jnp.where(left, store[found[k]], store[found[k + 1]])
                for k in range(0, len(sources), 2)
            ],
            axis=1,
        )
        for n in range(2):
            put(i, n, product(x, tiles, store, sources, n))


def cubes(tiles, store, squares_ref, put):
    for i in range(HALF):
        cube = None
        for k in range(2):
            g = jnp.concatenate([store[tiles[0, i * 8 + 4 * k + b]] for b in range(4)], axis=0)
            part = jnp.dot(
                squares_ref[i, :, k * 256 : (k + 1) * 256], g, preferred_element_type=jnp.float32
            )
            cube = part if cube is None else cube + part
        purified = 3.0 * squares_ref[i, :, 0:128].astype(jnp.float32) - 2.0 * cube
        put(i, purified[:, :64].astype(jnp.bfloat16))


def rounded(squares_ref, before=None):
    def put(i, n, total):
        at = slice(n * 256, (n + 1) * 256)
        if before is not None:
            total = total + before[i, :, at]
        squares_ref[i, :, at] = total.astype(jnp.bfloat16)

    return put


def waits_for_near():
    return (lax.axis_index("rows") == 0) & (lax.axis_index("rep") != 0)


def waits():
    return waits_for_near() | (lax.axis_index("rows") == 1)


def pack_kernel(
    x_ref,
    cols_in,
    counts_in,
    near_ref,
    far_ref,
    lists_ref,
    store,
    early_ref,
    near_rows,
    far_rows,
    near_sems,
    far_sems,
    cols_ref,
    counts_ref,
    own_sems,
):
    me = lax.axis_index("rows")
    core = lax.rem(me, 2)
    late = me == lax.axis_size("rows") - 1
    near = from_pieces(x_ref, near_rows, near_sems, (core * HALF, core * HALF + PIECE))
    far = from_pieces(x_ref, far_rows, far_sems, ((1 - core) * HALF, (1 - core) * HALF + PIECE))
    for copy in near:
        copy.start()

    @pl.when(jnp.logical_not(late))
    def _():
        for copy in far:
            copy.start()

    near_ref[HALF * 4 * TILE :, :] = jnp.zeros((PAD, 128), jnp.bfloat16)
    pack(near, near_rows, near_ref)

    @pl.when(jnp.logical_not(late))
    def _():
        pack(far, far_rows, far_ref)

    @pl.when(waits())
    def _():
        own(near_ref, far_ref, cols_in, counts_in, lists_ref, store, cols_ref, counts_ref, own_sems)

        def put(i, n, total):
            early_ref[i, :, n * 256 : (n + 1) * 256] = total

        squares(lists_ref[EARLY], store, 1, put)


def own_kernel(near_ref, far_ref, cols_in, counts_in, _, __, lists_ref, store, cols_ref, counts_ref, sems):
    @pl.when(jnp.logical_not(waits()))
    def _():
        own(near_ref, far_ref, cols_in, counts_in, lists_ref, store, cols_ref, counts_ref, sems)


def far_kernel(lists_ref, halo_ref, _, out_ref, store, squares_ref):
    me = lax.axis_index("rows")
    core = lax.rem(me, 2)
    fill(store, 3 * (1 - core), halo_ref)

    def put(i, block):
        out_ref[i] = block

    @pl.when(me != 1)
    def _():
        tiles = half_list(lists_ref, 2 - core)
        squares(tiles, store, 2 - core, rounded(squares_ref))
        cubes(tiles, store, squares_ref, put)


def near_kernel(lists_ref, halo_ref, far_in, early_ref, _, out_ref, store, squares_ref, near, far, sems):
    me = lax.axis_index("rows")
    core = lax.rem(me, 2)
    near_at = out_ref.at[pl.ds(core * HALF, HALF), 0]
    far_at = out_ref.at[pl.ds((1 - core) * HALF, HALF), 0]
    near_out = pltpu.make_async_copy(near, near_at, sems.at[0])
    far_out = pltpu.make_async_copy(far_in, far_at, sems.at[1])
    late_out = pltpu.make_async_copy(far, far_at, sems.at[1])

    @pl.when(me != 1)
    def _():
        far_out.start()

    fill(store, 3 * core, halo_ref)

    def put(i, block):
        near[i] = block

    @pl.when(waits_for_near())
    def _():
        low_halo_squares(lists_ref, store, rounded(squares_ref, early_ref))
        cubes(lists_ref[ALL], store, squares_ref, put)

    @pl.when(jnp.logical_not(waits_for_near()))
    def _():
        tiles = half_list(lists_ref, 1 + core)
        squares(tiles, store, 1 + core, rounded(squares_ref))
        cubes(tiles, store, squares_ref, put)

    near_out.start()

    @pl.when(me == 1)
    def _():
        def put_far(i, block):
            far[i] = block

        low_halo_squares(lists_ref, store, rounded(squares_ref, early_ref))
        cubes(lists_ref[ALL], store, squares_ref, put_far)
        late_out.start()
        late_out.wait()

    @pl.when(me != 1)
    def _():
        far_out.wait()

    near_out.wait()


def vmem():
    return pl.BlockSpec(memory_space=pltpu.VMEM)


def hbm():
    return pl.BlockSpec(memory_space=pltpu.HBM)


def call(kernel, name, args, in_specs, out_shape, out_specs, scratch_shapes=(), aliases=None):
    return pl.pallas_call(
        kernel,
        out_shape=out_shape,
        in_specs=in_specs,
        out_specs=out_specs,
        scratch_shapes=scratch_shapes,
        input_output_aliases=aliases or {},
        compiler_params=pltpu.CompilerParams(vmem_limit_bytes=16 * 1024 * 1024),
        cost_estimate=pl.CostEstimate(flops=0, bytes_accessed=0, transcendentals=0),
        name=name,
    )(*args)


def local(block_values, pattern_cols, pattern_counts):
    count = lax.axis_size("rows")
    to_core = [(i, i ^ 1) for i in range(count)]
    to_chip = [(i, (i + 1 if i % 2 else i - 1) % count) for i in range(count)]
    bf16, i32 = jnp.bfloat16, jnp.int32
    block_values = pltpu.with_memory_space_constraint(block_values, pltpu.HBM)
    rows = [pltpu.VMEM((HALF, 8, 64, 64), bf16)]
    sems = [pltpu.SemaphoreType.DMA((HALF // PIECE,))]
    packed = [jax.ShapeDtypeStruct((HALF * 4 * TILE + pad, 128), bf16) for pad in (PAD, 0)]
    cols, counts = pattern_cols.T, pattern_counts.reshape(-1, 128)
    cols, counts = (pltpu.with_memory_space_constraint(x, pltpu.HBM) for x in (cols, counts))
    pattern = [pltpu.VMEM(cols.shape, i32), pltpu.VMEM(counts.shape, i32), pltpu.SemaphoreType.DMA((2,))]
    stored = [jax.ShapeDtypeStruct(LISTS, i32), jax.ShapeDtypeStruct(STORE, bf16)]
    near, far, lists, store, early = call(
        pack_kernel,
        "pack",
        [block_values, cols, counts],
        [hbm()] * 3,
        packed + stored + [jax.ShapeDtypeStruct((HALF, 64, 512), jnp.float32)],
        [vmem()] * 5,
        rows * 2 + sems * 2 + pattern,
    )
    far = call(
        rest_kernel,
        "rest",
        [block_values, far],
        [hbm(), vmem()],
        packed[1],
        vmem(),
        rows + sems,
        {1: 0},
    )
    near_halo = lax.ppermute(near, "rows", to_chip)
    far_halo = lax.ppermute(far, "rows", to_core)
    lists, store = call(
        own_kernel,
        "own",
        [near, far, cols, counts, lists, store],
        [vmem(), vmem(), hbm(), hbm(), vmem(), vmem()],
        stored,
        [vmem()] * 2,
        pattern,
        {4: 0, 5: 1},
    )
    scratch = [pltpu.VMEM((HALF, 64, 512), bf16)]
    far_result, store = call(
        far_kernel,
        "far_half",
        [lists, far_halo, store],
        [vmem()] * 3,
        [jax.ShapeDtypeStruct((HALF, 64, 64), bf16), stored[1]],
        [vmem()] * 2,
        scratch,
        {2: 1},
    )
    result, _ = call(
        near_kernel,
        "near_half",
        [lists, near_halo, far_result, early, store],
        [vmem()] * 5,
        [jax.ShapeDtypeStruct((2 * HALF, 1, 64, 64), bf16), stored[1]],
        [hbm(), vmem()],
        scratch + [pltpu.VMEM((HALF, 64, 64), bf16)] * 2 + [pltpu.SemaphoreType.DMA((2,))],
        {4: 1},
    )
    return result


def solution(mesh):
    in_specs = (P("rows", None, None, None), P(), P())
    out_specs = P("rows", "rep", None, None)
    return jax.shard_map(local, mesh=mesh, in_specs=in_specs, out_specs=out_specs, check_vma=False)
```

```python
import jax
import jax.numpy as jnp
from jax import lax
from jax.experimental import pallas as pl
from jax.experimental.pallas import tpu as pltpu
from jax.sharding import PartitionSpec as P

HALF = 8
PIECE = 4
WINDOW = 32
TILE = 64
PAD = 16
GROUP = 8
ZERO_TILE = WINDOW * GROUP
STORE = (ZERO_TILE + 1, TILE, 128)
ALL, EARLY, LOW, LOW_X = range(4)
LISTS = (4, 8, 128)


def fill(store, chunk, ref):
    for row in range(HALF):
        base = (chunk * HALF + row) * GROUP
        for pair in range(4):
            tile = ref[pl.ds((row * 4 + pair) * TILE, TILE), :]
            store[base + pair] = tile
            store[base + 4 + pair] = pltpu.roll(tile, 64, 1)


def from_pieces(x_ref, rows, sems, starts):
    return [
        pltpu.make_async_copy(x_ref.at[pl.ds(start, PIECE)], rows.at[pl.ds(n * PIECE, PIECE)], sems.at[n])
        for n, start in enumerate(starts)
    ]


def pack(copies, rows, out_ref):
    for n, copy in enumerate(copies):
        copy.wait()
        for row in range(n * PIECE, (n + 1) * PIECE):
            for pair in range(4):
                at = pl.ds((row * 4 + pair) * TILE, TILE)
                blocks = [rows[row, 2 * pair + side] for side in range(2)]
                out_ref[at, :] = jnp.concatenate(blocks, axis=1)


def rest_kernel(x_ref, _, far_ref, far_rows, far_sems):
    me = lax.axis_index("rows")
    core = lax.rem(me, 2)

    @pl.when(me == lax.axis_size("rows") - 1)
    def _():
        far = from_pieces(x_ref, far_rows, far_sems, ((1 - core) * HALF, (1 - core) * HALF + PIECE))
        for copy in far:
            copy.start()
        pack(far, far_rows, far_ref)


def own(near_ref, far_ref, cols_in, counts_in, lists_ref, store, cols_ref, counts_ref, sems):
    copies = [
        pltpu.make_async_copy(cols_in, cols_ref, sems.at[0]),
        pltpu.make_async_copy(counts_in, counts_ref, sems.at[1]),
    ]
    for copy in copies:
        copy.start()
    core = lax.rem(lax.axis_index("rows"), 2)
    zeros = jnp.zeros((TILE, 128), jnp.bfloat16)
    store[ZERO_TILE] = zeros
    fill(store, 1 + core, near_ref)
    fill(store, 2 - core, far_ref)
    for copy in copies:
        copy.wait()
    total = cols_ref.shape[1]
    chunks = total // 128
    start = lax.rem(lax.axis_index("rows") * (2 * HALF) + (total - HALF), total)
    first = lax.div(start, 128)
    second = lax.rem(first + 1, chunks)
    shift = lax.rem(256 - lax.rem(start, 128), 256)

    def window(get):
        both = jnp.concatenate([get(first), get(second)], axis=1)
        return pltpu.roll(both, shift, 1)[:, :128]

    cols = window(lambda k: cols_ref[:, pl.ds(pl.multiple_of(k * 128, 128), 128)])
    counts = window(lambda k: jnp.broadcast_to(counts_ref[pl.ds(k, 1), :], (8, 128)))
    relative = cols - start
    relative = jnp.where(relative < 0, relative + total, relative)
    slot = lax.broadcasted_iota(jnp.int32, (8, 128), 0)
    lane = lax.broadcasted_iota(jnp.int32, (8, 128), 1)
    live = (slot < counts) & (lane < WINDOW) & (relative < WINDOW)
    columns = jnp.where(live, relative, -1)
    side = (slot % 2) * 4 + slot // 2
    mine = lax.axis_index("rep")

    def at_lanes(which):
        return jnp.take_along_axis(columns, which, axis=1, mode="promise_in_bounds")

    def highest(x):
        return jnp.broadcast_to(jnp.max(x, axis=0, keepdims=True), (8, 128))

    def tiles(own, row):
        found = at_lanes(jnp.maximum(row, 0))
        result = jnp.full((8, 128), ZERO_TILE, jnp.int32)
        for q in range(8):
            wanted = highest(jnp.where(slot == (mine ^ q), own, -1))
            match = (found == wanted) & (wanted >= 0) & (row >= 0)
            tile = highest(jnp.where(match, row * GROUP + (side ^ (q % 2 * 4)), -1))
            result = jnp.where((slot == q) & (tile >= 0), tile, result)
        return result

    own_row = HALF + lane // 8
    own_columns = at_lanes(own_row)
    source = highest(jnp.where(slot == ((lane % 8) ^ mine), own_columns, -1))
    everything = tiles(own_columns, source)
    lists_ref[ALL] = everything
    lists_ref[EARLY] = jnp.where(source < HALF, ZERO_TILE, everything)
    lists_ref[LOW] = tiles(own_columns, lane % 8)
    right = (lane % 8 + lane // 8) % 2 * 4
    low_x = highest(jnp.where(own_columns == lane % 8, own_row * GROUP + (side ^ right), -1))
    lists_ref[LOW_X] = jnp.where(low_x >= 0, low_x, ZERO_TILE)


def half_list(lists_ref, center):
    return jnp.where(center == 1, lists_ref[ALL], pltpu.roll(lists_ref[ALL], 64, 1))


def product(x, tiles, store, sources, n):
    left = lax.broadcasted_iota(jnp.int16, (TILE, 128), 1) < 64

    def tile(p, b):
        if b is None:
            return jnp.zeros((TILE, 128), jnp.bfloat16)
        return jnp.where(left, store[tiles[2 * p, b]], store[tiles[2 * p + 1, b]])

    total = None
    for k in range(0, len(sources), 4):
        g = jnp.concatenate(
            [
                jnp.concatenate([tile(2 * n + j, b) for j in range(2)], axis=1)
                for b in sources[k : k + 4]
            ],
            axis=0,
        )
        part = jnp.dot(x[:, k * 64 : (k + 4) * 64], g, preferred_element_type=jnp.float32)
        total = part if total is None else total + part
    return total


def squares(tiles, store, center, put):
    mine = lax.axis_index("rep")
    for i in range(HALF):
        at = (center * HALF + i) * GROUP + lax.rem(mine, 2) * 4
        x = jnp.concatenate([store[at + (lax.div(mine, 2) ^ p)] for p in range(4)], axis=1)
        for n in range(2):
            put(i, n, product(x, tiles, store, [i * 8 + b for b in range(8)], n))


def low_halo_sources(i):
    return [i * 8 + w for w in range(i, HALF)] + [None] * (i % 2)


def low_halo_left(lists_ref, store, out_ref):
    own_tiles = lists_ref[LOW_X]
    left = lax.broadcasted_iota(jnp.int16, (TILE, 128), 1) < 64
    for i in range(HALF):
        found = [ZERO_TILE if b is None else own_tiles[0, b] for b in low_halo_sources(i)]
        for k in range(0, len(found), 2):
            out_ref[i, :, k * 64 : k * 64 + 128] = jnp.where(left, store[found[k]], store[found[k + 1]])


def low_halo_squares(lists_ref, left_ref, store, put):
    tiles = lists_ref[LOW]
    for i in range(HALF):
        sources = low_halo_sources(i)
        x = left_ref[i, :, : len(sources) * 64]
        for n in range(2):
            put(i, n, product(x, tiles, store, sources, n))


def cubes(tiles, store, squares_ref, put):
    for i in range(HALF):
        cube = None
        for k in range(2):
            g = jnp.concatenate([store[tiles[0, i * 8 + 4 * k + b]] for b in range(4)], axis=0)
            part = jnp.dot(
                squares_ref[i, :, k * 256 : (k + 1) * 256], g, preferred_element_type=jnp.float32
            )
            cube = part if cube is None else cube + part
        purified = 3.0 * squares_ref[i, :, 0:128].astype(jnp.float32) - 2.0 * cube
        put(i, purified[:, :64].astype(jnp.bfloat16))


def rounded(squares_ref, before=None):
    def put(i, n, total):
        at = slice(n * 256, (n + 1) * 256)
        if before is not None:
            total = total + before[i, :, at]
        squares_ref[i, :, at] = total.astype(jnp.bfloat16)

    return put


def waits_for_near():
    return (lax.axis_index("rows") == 0) & (lax.axis_index("rep") != 0)


def waits():
    return waits_for_near() | (lax.axis_index("rows") == 1)


def pack_kernel(
    x_ref,
    cols_in,
    counts_in,
    near_ref,
    far_ref,
    lists_ref,
    store,
    early_ref,
    left_ref,
    near_rows,
    far_rows,
    near_sems,
    far_sems,
    cols_ref,
    counts_ref,
    own_sems,
):
    me = lax.axis_index("rows")
    core = lax.rem(me, 2)
    late = me == lax.axis_size("rows") - 1
    near = from_pieces(x_ref, near_rows, near_sems, (core * HALF, core * HALF + PIECE))
    far = from_pieces(x_ref, far_rows, far_sems, ((1 - core) * HALF, (1 - core) * HALF + PIECE))
    for copy in near:
        copy.start()

    @pl.when(jnp.logical_not(late))
    def _():
        for copy in far:
            copy.start()

    near_ref[HALF * 4 * TILE :, :] = jnp.zeros((PAD, 128), jnp.bfloat16)
    pack(near, near_rows, near_ref)

    @pl.when(jnp.logical_not(late))
    def _():
        pack(far, far_rows, far_ref)

    @pl.when(waits())
    def _():
        own(near_ref, far_ref, cols_in, counts_in, lists_ref, store, cols_ref, counts_ref, own_sems)

        def put(i, n, total):
            early_ref[i, :, n * 256 : (n + 1) * 256] = total

        squares(lists_ref[EARLY], store, 1, put)
        low_halo_left(lists_ref, store, left_ref)


def own_kernel(near_ref, far_ref, cols_in, counts_in, _, __, lists_ref, store, cols_ref, counts_ref, sems):
    @pl.when(jnp.logical_not(waits()))
    def _():
        own(near_ref, far_ref, cols_in, counts_in, lists_ref, store, cols_ref, counts_ref, sems)


def far_kernel(lists_ref, halo_ref, _, out_ref, store, squares_ref):
    me = lax.axis_index("rows")
    core = lax.rem(me, 2)
    fill(store, 3 * (1 - core), halo_ref)

    def put(i, block):
        out_ref[i] = block

    @pl.when(me != 1)
    def _():
        tiles = half_list(lists_ref, 2 - core)
        squares(tiles, store, 2 - core, rounded(squares_ref))
        cubes(tiles, store, squares_ref, put)


def near_kernel(
    lists_ref, halo_ref, far_in, early_ref, left_ref, _, out_ref, store, squares_ref, near, far, sems
):
    me = lax.axis_index("rows")
    core = lax.rem(me, 2)
    near_at = out_ref.at[pl.ds(core * HALF, HALF), 0]
    far_at = out_ref.at[pl.ds((1 - core) * HALF, HALF), 0]
    near_out = pltpu.make_async_copy(near, near_at, sems.at[0])
    far_out = pltpu.make_async_copy(far_in, far_at, sems.at[1])
    late_out = pltpu.make_async_copy(far, far_at, sems.at[1])

    @pl.when(me != 1)
    def _():
        far_out.start()

    fill(store, 3 * core, halo_ref)

    def put(i, block):
        near[i] = block

    @pl.when(waits_for_near())
    def _():
        low_halo_squares(lists_ref, left_ref, store, rounded(squares_ref, early_ref))
        cubes(lists_ref[ALL], store, squares_ref, put)

    @pl.when(jnp.logical_not(waits_for_near()))
    def _():
        tiles = half_list(lists_ref, 1 + core)
        squares(tiles, store, 1 + core, rounded(squares_ref))
        cubes(tiles, store, squares_ref, put)

    near_out.start()

    @pl.when(me == 1)
    def _():
        def put_far(i, block):
            far[i] = block

        low_halo_squares(lists_ref, left_ref, store, rounded(squares_ref, early_ref))
        cubes(lists_ref[ALL], store, squares_ref, put_far)
        late_out.start()
        late_out.wait()

    @pl.when(me != 1)
    def _():
        far_out.wait()

    near_out.wait()


def vmem():
    return pl.BlockSpec(memory_space=pltpu.VMEM)


def hbm():
    return pl.BlockSpec(memory_space=pltpu.HBM)


def call(kernel, name, args, in_specs, out_shape, out_specs, scratch_shapes=(), aliases=None):
    return pl.pallas_call(
        kernel,
        out_shape=out_shape,
        in_specs=in_specs,
        out_specs=out_specs,
        scratch_shapes=scratch_shapes,
        input_output_aliases=aliases or {},
        compiler_params=pltpu.CompilerParams(vmem_limit_bytes=16 * 1024 * 1024),
        cost_estimate=pl.CostEstimate(flops=0, bytes_accessed=0, transcendentals=0),
        name=name,
    )(*args)


def local(block_values, pattern_cols, pattern_counts):
    count = lax.axis_size("rows")
    to_core = [(i, i ^ 1) for i in range(count)]
    to_chip = [(i, (i + 1 if i % 2 else i - 1) % count) for i in range(count)]
    bf16, i32 = jnp.bfloat16, jnp.int32
    block_values = pltpu.with_memory_space_constraint(block_values, pltpu.HBM)
    rows = [pltpu.VMEM((HALF, 8, 64, 64), bf16)]
    sems = [pltpu.SemaphoreType.DMA((HALF // PIECE,))]
    packed = [jax.ShapeDtypeStruct((HALF * 4 * TILE + pad, 128), bf16) for pad in (PAD, 0)]
    cols, counts = pattern_cols.T, pattern_counts.reshape(-1, 128)
    cols, counts = (pltpu.with_memory_space_constraint(x, pltpu.HBM) for x in (cols, counts))
    pattern = [pltpu.VMEM(cols.shape, i32), pltpu.VMEM(counts.shape, i32), pltpu.SemaphoreType.DMA((2,))]
    stored = [jax.ShapeDtypeStruct(LISTS, i32), jax.ShapeDtypeStruct(STORE, bf16)]
    near, far, lists, store, early, left = call(
        pack_kernel,
        "pack",
        [block_values, cols, counts],
        [hbm()] * 3,
        packed + stored + [jax.ShapeDtypeStruct((HALF, 64, 512), kind) for kind in (jnp.float32, bf16)],
        [vmem()] * 6,
        rows * 2 + sems * 2 + pattern,
    )
    far = call(
        rest_kernel,
        "rest",
        [block_values, far],
        [hbm(), vmem()],
        packed[1],
        vmem(),
        rows + sems,
        {1: 0},
    )
    near_halo = lax.ppermute(near, "rows", to_chip)
    far_halo = lax.ppermute(far, "rows", to_core)
    lists, store = call(
        own_kernel,
        "own",
        [near, far, cols, counts, lists, store],
        [vmem(), vmem(), hbm(), hbm(), vmem(), vmem()],
        stored,
        [vmem()] * 2,
        pattern,
        {4: 0, 5: 1},
    )
    scratch = [pltpu.VMEM((HALF, 64, 512), bf16)]
    far_result, store = call(
        far_kernel,
        "far_half",
        [lists, far_halo, store],
        [vmem()] * 3,
        [jax.ShapeDtypeStruct((HALF, 64, 64), bf16), stored[1]],
        [vmem()] * 2,
        scratch,
        {2: 1},
    )
    result, _ = call(
        near_kernel,
        "near_half",
        [lists, near_halo, far_result, early, left, store],
        [vmem()] * 6,
        [jax.ShapeDtypeStruct((2 * HALF, 1, 64, 64), bf16), stored[1]],
        [hbm(), vmem()],
        scratch + [pltpu.VMEM((HALF, 64, 64), bf16)] * 2 + [pltpu.SemaphoreType.DMA((2,))],
        {5: 1},
    )
    return result


def solution(mesh):
    in_specs = (P("rows", None, None, None), P(), P())
    out_specs = P("rows", "rep", None, None)
    return jax.shard_map(local, mesh=mesh, in_specs=in_specs, out_specs=out_specs, check_vma=False)
```

```python
import jax
import jax.numpy as jnp
from jax import lax
from jax.experimental import pallas as pl
from jax.experimental.pallas import tpu as pltpu
from jax.sharding import PartitionSpec as P

HALF = 8
PIECES = ((0, 6), (6, 2))
WINDOW = 32
TILE = 64
PAD = 16
GROUP = 8
ZERO_TILE = WINDOW * GROUP
STORE = (ZERO_TILE + 1, TILE, 128)
ALL, EARLY, LOW, LOW_X = range(4)
LISTS = (4, 8, 128)


def fill(store, chunk, ref):
    for row in range(HALF):
        base = (chunk * HALF + row) * GROUP
        for pair in range(4):
            tile = ref[pl.ds((row * 4 + pair) * TILE, TILE), :]
            store[base + pair] = tile
            store[base + 4 + pair] = pltpu.roll(tile, 64, 1)


def from_pieces(x_ref, rows, sems, base):
    return [
        pltpu.make_async_copy(x_ref.at[pl.ds(base + at, size)], rows.at[pl.ds(at, size)], sems.at[n])
        for n, (at, size) in enumerate(PIECES)
    ]


def pack(copies, rows, out_ref):
    for copy, (first, size) in zip(copies, PIECES):
        copy.wait()
        for row in range(first, first + size):
            for pair in range(4):
                at = pl.ds((row * 4 + pair) * TILE, TILE)
                blocks = [rows[row, 2 * pair + side] for side in range(2)]
                out_ref[at, :] = jnp.concatenate(blocks, axis=1)


def rest_kernel(x_ref, _, far_ref, far_rows, far_sems):
    me = lax.axis_index("rows")
    core = lax.rem(me, 2)

    @pl.when(me == lax.axis_size("rows") - 1)
    def _():
        far = from_pieces(x_ref, far_rows, far_sems, (1 - core) * HALF)
        for copy in far:
            copy.start()
        pack(far, far_rows, far_ref)


def own(near_ref, far_ref, cols_in, counts_in, lists_ref, store, cols_ref, counts_ref, sems):
    copies = [
        pltpu.make_async_copy(cols_in, cols_ref, sems.at[0]),
        pltpu.make_async_copy(counts_in, counts_ref, sems.at[1]),
    ]
    for copy in copies:
        copy.start()
    core = lax.rem(lax.axis_index("rows"), 2)
    zeros = jnp.zeros((TILE, 128), jnp.bfloat16)
    store[ZERO_TILE] = zeros
    fill(store, 1 + core, near_ref)
    fill(store, 2 - core, far_ref)
    for copy in copies:
        copy.wait()
    total = cols_ref.shape[1]
    chunks = total // 128
    start = lax.rem(lax.axis_index("rows") * (2 * HALF) + (total - HALF), total)
    first = lax.div(start, 128)
    second = lax.rem(first + 1, chunks)
    shift = lax.rem(256 - lax.rem(start, 128), 256)

    def window(get):
        both = jnp.concatenate([get(first), get(second)], axis=1)
        return pltpu.roll(both, shift, 1)[:, :128]

    cols = window(lambda k: cols_ref[:, pl.ds(pl.multiple_of(k * 128, 128), 128)])
    counts = window(lambda k: jnp.broadcast_to(counts_ref[pl.ds(k, 1), :], (8, 128)))
    relative = cols - start
    relative = jnp.where(relative < 0, relative + total, relative)
    slot = lax.broadcasted_iota(jnp.int32, (8, 128), 0)
    lane = lax.broadcasted_iota(jnp.int32, (8, 128), 1)
    live = (slot < counts) & (lane < WINDOW) & (relative < WINDOW)
    columns = jnp.where(live, relative, -1)
    side = (slot % 2) * 4 + slot // 2
    mine = lax.axis_index("rep")

    def at_lanes(which):
        return jnp.take_along_axis(columns, which, axis=1, mode="promise_in_bounds")

    def highest(x):
        return jnp.broadcast_to(jnp.max(x, axis=0, keepdims=True), (8, 128))

    def tiles(own, row):
        found = at_lanes(jnp.maximum(row, 0))
        result = jnp.full((8, 128), ZERO_TILE, jnp.int32)
        for q in range(8):
            wanted = highest(jnp.where(slot == (mine ^ q), own, -1))
            match = (found == wanted) & (wanted >= 0) & (row >= 0)
            tile = highest(jnp.where(match, row * GROUP + (side ^ (q % 2 * 4)), -1))
            result = jnp.where((slot == q) & (tile >= 0), tile, result)
        return result

    own_row = HALF + lane // 8
    own_columns = at_lanes(own_row)
    source = highest(jnp.where(slot == ((lane % 8) ^ mine), own_columns, -1))
    everything = tiles(own_columns, source)
    lists_ref[ALL] = everything
    lists_ref[EARLY] = jnp.where(source < HALF, ZERO_TILE, everything)
    lists_ref[LOW] = tiles(own_columns, lane % 8)
    right = (lane % 8 + lane // 8) % 2 * 4
    low_x = highest(jnp.where(own_columns == lane % 8, own_row * GROUP + (side ^ right), -1))
    lists_ref[LOW_X] = jnp.where(low_x >= 0, low_x, ZERO_TILE)


def half_list(lists_ref, center):
    return jnp.where(center == 1, lists_ref[ALL], pltpu.roll(lists_ref[ALL], 64, 1))


def product(x, tiles, store, sources, n):
    left = lax.broadcasted_iota(jnp.int16, (TILE, 128), 1) < 64

    def tile(p, b):
        if b is None:
            return jnp.zeros((TILE, 128), jnp.bfloat16)
        return jnp.where(left, store[tiles[2 * p, b]], store[tiles[2 * p + 1, b]])

    total = None
    for k in range(0, len(sources), 4):
        g = jnp.concatenate(
            [
                jnp.concatenate([tile(2 * n + j, b) for j in range(2)], axis=1)
                for b in sources[k : k + 4]
            ],
            axis=0,
        )
        part = jnp.dot(x[:, k * 64 : (k + 4) * 64], g, preferred_element_type=jnp.float32)
        total = part if total is None else total + part
    return total


def squares(tiles, store, center, put):
    mine = lax.axis_index("rep")
    for i in range(HALF):
        at = (center * HALF + i) * GROUP + lax.rem(mine, 2) * 4
        x = jnp.concatenate([store[at + (lax.div(mine, 2) ^ p)] for p in range(4)], axis=1)
        for n in range(2):
            put(i, n, product(x, tiles, store, [i * 8 + b for b in range(8)], n))


def low_halo_sources(i):
    return [i * 8 + w for w in range(i, HALF)] + [None] * (i % 2)


def low_halo_left(lists_ref, store, out_ref):
    own_tiles = lists_ref[LOW_X]
    left = lax.broadcasted_iota(jnp.int16, (TILE, 128), 1) < 64
    for i in range(HALF):
        found = [ZERO_TILE if b is None else own_tiles[0, b] for b in low_halo_sources(i)]
        for k in range(0, len(found), 2):
            out_ref[i, :, k * 64 : k * 64 + 128] = jnp.where(left, store[found[k]], store[found[k + 1]])


def low_halo_squares(lists_ref, left_ref, store, put):
    tiles = lists_ref[LOW]
    for i in range(HALF):
        sources = low_halo_sources(i)
        x = left_ref[i, :, : len(sources) * 64]
        for n in range(2):
            put(i, n, product(x, tiles, store, sources, n))


def cubes(tiles, store, squares_ref, put):
    for i in range(HALF):
        cube = None
        for k in range(2):
            g = jnp.concatenate([store[tiles[0, i * 8 + 4 * k + b]] for b in range(4)], axis=0)
            part = jnp.dot(
                squares_ref[i, :, k * 256 : (k + 1) * 256], g, preferred_element_type=jnp.float32
            )
            cube = part if cube is None else cube + part
        purified = 3.0 * squares_ref[i, :, 0:128].astype(jnp.float32) - 2.0 * cube
        put(i, purified[:, :64].astype(jnp.bfloat16))


def rounded(squares_ref, before=None):
    def put(i, n, total):
        at = slice(n * 256, (n + 1) * 256)
        if before is not None:
            total = total + before[i, :, at]
        squares_ref[i, :, at] = total.astype(jnp.bfloat16)

    return put


def waits_for_near():
    return (lax.axis_index("rows") == 0) & (lax.axis_index("rep") != 0)


def waits():
    return waits_for_near() | (lax.axis_index("rows") == 1)


def pack_kernel(
    x_ref,
    cols_in,
    counts_in,
    near_ref,
    far_ref,
    lists_ref,
    store,
    early_ref,
    left_ref,
    near_rows,
    far_rows,
    near_sems,
    far_sems,
    cols_ref,
    counts_ref,
    own_sems,
):
    me = lax.axis_index("rows")
    core = lax.rem(me, 2)
    late = me == lax.axis_size("rows") - 1
    near = from_pieces(x_ref, near_rows, near_sems, core * HALF)
    far = from_pieces(x_ref, far_rows, far_sems, (1 - core) * HALF)
    for copy in near:
        copy.start()

    @pl.when(jnp.logical_not(late))
    def _():
        for copy in far:
            copy.start()

    near_ref[HALF * 4 * TILE :, :] = jnp.zeros((PAD, 128), jnp.bfloat16)
    pack(near, near_rows, near_ref)

    @pl.when(jnp.logical_not(late))
    def _():
        pack(far, far_rows, far_ref)

    @pl.when(waits())
    def _():
        own(near_ref, far_ref, cols_in, counts_in, lists_ref, store, cols_ref, counts_ref, own_sems)

        def put(i, n, total):
            early_ref[i, :, n * 256 : (n + 1) * 256] = total

        squares(lists_ref[EARLY], store, 1, put)
        low_halo_left(lists_ref, store, left_ref)


def own_kernel(near_ref, far_ref, cols_in, counts_in, _, __, lists_ref, store, cols_ref, counts_ref, sems):
    @pl.when(jnp.logical_not(waits()))
    def _():
        own(near_ref, far_ref, cols_in, counts_in, lists_ref, store, cols_ref, counts_ref, sems)


def far_kernel(lists_ref, halo_ref, _, out_ref, store, squares_ref):
    me = lax.axis_index("rows")
    core = lax.rem(me, 2)
    fill(store, 3 * (1 - core), halo_ref)

    def put(i, block):
        out_ref[i] = block

    @pl.when(me != 1)
    def _():
        tiles = half_list(lists_ref, 2 - core)
        squares(tiles, store, 2 - core, rounded(squares_ref))
        cubes(tiles, store, squares_ref, put)


def near_kernel(
    lists_ref, halo_ref, far_in, early_ref, left_ref, _, out_ref, store, squares_ref, near, far, sems
):
    me = lax.axis_index("rows")
    core = lax.rem(me, 2)
    near_at = out_ref.at[pl.ds(core * HALF, HALF), 0]
    far_at = out_ref.at[pl.ds((1 - core) * HALF, HALF), 0]
    near_out = pltpu.make_async_copy(near, near_at, sems.at[0])
    far_out = pltpu.make_async_copy(far_in, far_at, sems.at[1])
    late_out = pltpu.make_async_copy(far, far_at, sems.at[1])

    @pl.when(me != 1)
    def _():
        far_out.start()

    fill(store, 3 * core, halo_ref)

    def put(i, block):
        near[i] = block

    @pl.when(waits_for_near())
    def _():
        low_halo_squares(lists_ref, left_ref, store, rounded(squares_ref, early_ref))
        cubes(lists_ref[ALL], store, squares_ref, put)

    @pl.when(jnp.logical_not(waits_for_near()))
    def _():
        tiles = half_list(lists_ref, 1 + core)
        squares(tiles, store, 1 + core, rounded(squares_ref))
        cubes(tiles, store, squares_ref, put)

    near_out.start()

    @pl.when(me == 1)
    def _():
        def put_far(i, block):
            far[i] = block

        low_halo_squares(lists_ref, left_ref, store, rounded(squares_ref, early_ref))
        cubes(lists_ref[ALL], store, squares_ref, put_far)
        late_out.start()
        late_out.wait()

    @pl.when(me != 1)
    def _():
        far_out.wait()

    near_out.wait()


def vmem():
    return pl.BlockSpec(memory_space=pltpu.VMEM)


def hbm():
    return pl.BlockSpec(memory_space=pltpu.HBM)


def call(kernel, name, args, in_specs, out_shape, out_specs, scratch_shapes=(), aliases=None):
    return pl.pallas_call(
        kernel,
        out_shape=out_shape,
        in_specs=in_specs,
        out_specs=out_specs,
        scratch_shapes=scratch_shapes,
        input_output_aliases=aliases or {},
        compiler_params=pltpu.CompilerParams(vmem_limit_bytes=16 * 1024 * 1024),
        cost_estimate=pl.CostEstimate(flops=0, bytes_accessed=0, transcendentals=0),
        name=name,
    )(*args)


def local(block_values, pattern_cols, pattern_counts):
    count = lax.axis_size("rows")
    to_core = [(i, i ^ 1) for i in range(count)]
    to_chip = [(i, (i + 1 if i % 2 else i - 1) % count) for i in range(count)]
    bf16, i32 = jnp.bfloat16, jnp.int32
    block_values = pltpu.with_memory_space_constraint(block_values, pltpu.HBM)
    rows = [pltpu.VMEM((HALF, 8, 64, 64), bf16)]
    sems = [pltpu.SemaphoreType.DMA((len(PIECES),))]
    packed = [jax.ShapeDtypeStruct((HALF * 4 * TILE + pad, 128), bf16) for pad in (PAD, 0)]
    cols, counts = pattern_cols.T, pattern_counts.reshape(-1, 128)
    cols, counts = (pltpu.with_memory_space_constraint(x, pltpu.HBM) for x in (cols, counts))
    pattern = [pltpu.VMEM(cols.shape, i32), pltpu.VMEM(counts.shape, i32), pltpu.SemaphoreType.DMA((2,))]
    stored = [jax.ShapeDtypeStruct(LISTS, i32), jax.ShapeDtypeStruct(STORE, bf16)]
    near, far, lists, store, early, left = call(
        pack_kernel,
        "pack",
        [block_values, cols, counts],
        [hbm()] * 3,
        packed + stored + [jax.ShapeDtypeStruct((HALF, 64, 512), kind) for kind in (jnp.float32, bf16)],
        [vmem()] * 6,
        rows * 2 + sems * 2 + pattern,
    )
    far = call(
        rest_kernel,
        "rest",
        [block_values, far],
        [hbm(), vmem()],
        packed[1],
        vmem(),
        rows + sems,
        {1: 0},
    )
    near_halo = lax.ppermute(near, "rows", to_chip)
    far_halo = lax.ppermute(far, "rows", to_core)
    lists, store = call(
        own_kernel,
        "own",
        [near, far, cols, counts, lists, store],
        [vmem(), vmem(), hbm(), hbm(), vmem(), vmem()],
        stored,
        [vmem()] * 2,
        pattern,
        {4: 0, 5: 1},
    )
    scratch = [pltpu.VMEM((HALF, 64, 512), bf16)]
    far_result, store = call(
        far_kernel,
        "far_half",
        [lists, far_halo, store],
        [vmem()] * 3,
        [jax.ShapeDtypeStruct((HALF, 64, 64), bf16), stored[1]],
        [vmem()] * 2,
        scratch,
        {2: 1},
    )
    result, _ = call(
        near_kernel,
        "near_half",
        [lists, near_halo, far_result, early, left, store],
        [vmem()] * 6,
        [jax.ShapeDtypeStruct((2 * HALF, 1, 64, 64), bf16), stored[1]],
        [hbm(), vmem()],
        scratch + [pltpu.VMEM((HALF, 64, 64), bf16)] * 2 + [pltpu.SemaphoreType.DMA((2,))],
        {5: 1},
    )
    return result


def solution(mesh):
    in_specs = (P("rows", None, None, None), P(), P())
    out_specs = P("rows", "rep", None, None)
    return jax.shard_map(local, mesh=mesh, in_specs=in_specs, out_specs=out_specs, check_vma=False)
```
